128 devices in a mesh: dp: 16 (over y_hi, z, core), blk: 8 (over x, y_lo).
Axes of the slice: x: 4, y: 4 (y_hi: 2, y_lo: 2; y = y_hi * 2 + y_lo), z: 4, core: 2. Of those that a mesh axis runs over, the one named last changes fastest.
Arguments:
- layer_input: bfloat16 [16, 1024, 768], P('dp', 'blk'), may hold values from -6 to 6
- out_grad: bfloat16 [16, 1024, 768], P('dp', 'blk'), may hold values from -6 to 6
- lengths: int32 [16, 4], P('dp'), may hold values from 3 to 1015, as said below
- keep: int32 [2, 16, 4], P(None, 'dp'), may hold values 0 or 1
- ln1_gain: float32 [768], replicated, may hold values from 0.5 to 1.5
- ln1_bias: float32 [768], replicated, may hold values from -3 to 3
- w_qkv: bfloat16 [768, 2304], replicated, may hold values from -0.21875 to 0.21875
- b_query: float32 [768], replicated, may hold values from -3 to 3
- b_value: float32 [768], replicated, may hold values from -3 to 3
- w_proj: bfloat16 [768, 768], replicated, may hold values from -1.25 to 1.25
- b_proj: float32 [768], replicated, may hold values from -2 to 2
- ln2_gain: float32 [768], replicated, may hold values from 0.5 to 1.5
- ln2_bias: float32 [768], replicated, may hold values from -3 to 3
- w_fc1: bfloat16 [768, 3072], replicated, may hold values from -0.21875 to 0.21875
- b_fc1: float32 [3072], replicated, may hold values from -3 to 3
- w_fc2: bfloat16 [3072, 768], replicated, may hold values from -0.109375 to 0.109375
- b_fc2: float32 [768], replicated, may hold values from -2 to 2
Outputs:
- output: bfloat16 [16, 1024, 768], P('dp', 'blk')
- x_grad: bfloat16 [16, 1024, 768], P('dp', 'blk')
- grad_ln1_gain: float32 [768], replicated
- grad_ln1_bias: float32 [768], replicated
- grad_w_qkv: float32 [768, 2304], replicated
- grad_b_query: float32 [768], replicated
- grad_b_value: float32 [768], replicated
- grad_w_proj: float32 [768, 768], replicated
- grad_b_proj: float32 [768], replicated
- grad_ln2_gain: float32 [768], replicated
- grad_ln2_bias: float32 [768], replicated
- grad_w_fc1: float32 [768, 3072], replicated
- grad_b_fc1: float32 [3072], replicated
- grad_w_fc2: float32 [3072, 768], replicated
- grad_b_fc2: float32 [768], replicated
The draws below stay inside these ranges and needn't reach their ends.
Inputs may be any that keep to these rules, and one draw needn't show every extreme that they name: Each row holds 4 images of 3 or more tokens laid out in order from the row's start; their lengths sum to at most 1024, the remaining tokens are padding.
All inputs are finite; a program needn't handle non-finite values. No bound on the sum of `keep` on one device may be relied on, other than what follows from the above.
Results may differ from the reference program's by a relative error of at most 0.014.
Values may be sent and summed in bfloat16 or wider, within the bound.
No kernel may reach another device: no remote copies, remote signals or barrier semaphores. Data moves between devices by JAX's collectives and lax.ppermute only.
A program may use at most 192 MiB of HBM per device.

```python
import jax
import jax.numpy as jnp
from jax import lax

D = 768
HEADS = 12
HEAD_DIM = 64
FF = 3072
L = 1024
IMGS = 4
TOK_DEV = 128
ROWS = 16


def draw_lengths(key, part):
    key = jax.random.fold_in(key, 11)
    key_small, key_pad, key_big, key_row = jax.random.split(key, 4)
    quarter = TOK_DEV // 4
    small = jax.random.randint(key_small, (ROWS, IMGS), 3, quarter + 1)
    padding = jax.random.randint(key_pad, (ROWS, 1), 0, quarter + 1)
    full_row = jax.random.randint(key_row, (), 0, ROWS)
    is_full = (jnp.arange(ROWS, dtype=jnp.int32) == full_row)[:, None]
    small = jnp.where(is_full, 3, small)
    padding = jnp.where(is_full, 0, padding)
    chosen = jax.random.randint(key_big, (ROWS, 1), 0, IMGS)
    is_big = jnp.arange(IMGS, dtype=jnp.int32)[None, :] == chosen
    others = jnp.sum(jnp.where(is_big, 0, small), axis=1, keepdims=True)
    return jnp.where(is_big, L - others - padding, small).astype(jnp.int32)


def plant(values, stream_key, low, high):
    spot = [jax.random.randint(jax.random.fold_in(stream_key, axis), (), 0, length) for axis, length in enumerate(values.shape)]
    longest = values.shape.index(max(values.shape))
    beside = spot[:longest] + [(spot[longest] + 1) % values.shape[longest]] + spot[longest + 1:]
    return values.at[tuple(spot)].set(low).at[tuple(beside)].set(high)


def block_scale(key, shape, cuts, least, largest):
    def one(axis_at, parts):
        steps = jax.random.uniform(jax.random.fold_in(jax.random.fold_in(key, 6), axis_at), (parts,), jnp.float32, least / len(cuts), largest / len(cuts))
        return jnp.repeat(jnp.exp(steps), shape[axis_at] // parts).reshape((-1,) + (1,) * (len(shape) - axis_at - 1))

    level = one(*cuts[0])
    for cut in cuts[1:]:
        level = level * one(*cut)
    return level


def noise(rng, extent, deviation, limit, shards=(), held_as=jnp.bfloat16):
    array = deviation * jax.random.normal(rng, extent, jnp.float32)
    if shards:
        array = array * block_scale(rng, extent, shards, -0.22, 0.18)
    return jnp.clip(array, -limit, limit).astype(held_as)


def setup_inputs(seed: int = 0) -> dict:
    seeds = jax.random.split(jax.random.key(seed), 18)
    layer_input = noise(seeds[0], (ROWS, L, D), 1.0, 6.0, ((0, 16), (1, 8)))
    out_grad = noise(seeds[1], (ROWS, L, D), 1.0, 6.0, ((0, 16), (1, 8)))
    lengths = draw_lengths(jax.random.fold_in(seeds[17], 71), 0)
    keep = plant((jax.random.randint(seeds[3], (2, ROWS, IMGS), 0, 10) < 9).astype(jnp.int32), jax.random.fold_in(seeds[3], 1), 0, 1)
    ln1_gain = jnp.clip(1.0 + 0.1 * jax.random.normal(seeds[4], (D,), jnp.float32), 0.5, 1.5)
    ln1_bias = noise(seeds[5], (D,), 0.5, 3.0, (), jnp.float32)
    w_qkv = noise(seeds[6], (D, 3 * D), D ** -0.5, 0.21875)
    b_query = noise(seeds[7], (D,), 0.5, 3.0, (), jnp.float32)
    b_value = noise(seeds[8], (D,), 0.5, 3.0, (), jnp.float32)
    w_proj = noise(seeds[9], (D, D), (D // 32) ** -0.5, 1.25)
    b_proj = noise(seeds[10], (D,), 0.3, 2.0, (), jnp.float32)
    ln2_gain = jnp.clip(1.0 + 0.1 * jax.random.normal(seeds[11], (D,), jnp.float32), 0.5, 1.5)
    ln2_bias = noise(seeds[12], (D,), 0.5, 3.0, (), jnp.float32)
    w_fc1 = noise(seeds[13], (D, FF), D ** -0.5, 0.21875)
    b_fc1 = noise(seeds[14], (FF,), 0.5, 3.0, (), jnp.float32)
    w_fc2 = noise(seeds[15], (FF, D), FF ** -0.5, 0.109375)
    b_fc2 = noise(seeds[16], (D,), 0.3, 2.0, (), jnp.float32)
    return {"layer_input": layer_input, "out_grad": out_grad, "lengths": lengths, "keep": keep, "ln1_gain": ln1_gain, "ln1_bias": ln1_bias, "w_qkv": w_qkv, "b_query": b_query, "b_value": b_value, "w_proj": w_proj, "b_proj": b_proj, "ln2_gain": ln2_gain, "ln2_bias": ln2_bias, "w_fc1": w_fc1, "b_fc1": b_fc1, "w_fc2": w_fc2, "b_fc2": b_fc2}


@jax.custom_vjp
def low(v):
    return lax.optimization_barrier(v.astype(jnp.bfloat16)).astype(jnp.float32)

@jax.custom_vjp
def low_back(v):
    return v

def low_keep(v):
    return (low(v), None)

def low_pass(kept, grad):
    return (grad,)

def back_keep(v):
    return (v, None)

def back_low(kept, grad):
    return (low(grad),)
low.defvjp(low_keep, low_pass)
low_back.defvjp(back_keep, back_low)
eps_norm = 1e-06
drop_scale = 1.0 / 0.9
far_below = -1e+30

def matmul(left, right):
    return jnp.dot(left, right, precision=lax.Precision.HIGHEST, preferred_element_type=jnp.float32)

def layer_norm(values, gain, shift):
    mean = lax.optimization_barrier(jnp.mean(values, axis=-1, keepdims=True))
    centred = values - mean
    variance = lax.optimization_barrier(jnp.mean(centred * centred, axis=-1, keepdims=True))
    return centred * lax.rsqrt(variance + eps_norm) * gain + shift

def token_tables(lengths, keep):
    ends = jnp.cumsum(lengths, axis=1)
    places = jnp.arange(L, dtype=jnp.int32)
    image_id = lax.optimization_barrier(jnp.sum((ends[:, None, :] <= places[None, :, None]).astype(jnp.int32), axis=2))
    onehot = (image_id[:, :, None] == jnp.arange(IMGS, dtype=jnp.int32)[None, None, :]).astype(jnp.float32)
    keeps = jnp.einsum('rti,bri->brt', onehot, keep.astype(jnp.float32)) * drop_scale
    return (image_id, keeps)

def row_layer(params, x_row, id_row, keep_attn, keep_mlp):
    gain_one, bias_one, w_qkv, b_query, b_value, w_proj, b_proj, gain_two, bias_two, w_fc1, b_fc1, w_fc2, b_fc2 = params
    h_one = low(layer_norm(x_row, gain_one, bias_one))
    qkv_bias = jnp.concatenate([b_query, jnp.zeros_like(b_query), b_value])
    qkv = low(low_back(matmul(h_one, w_qkv) + qkv_bias))
    query = qkv[:, :D].reshape(L, HEADS, HEAD_DIM)
    keys = qkv[:, D:2 * D].reshape(L, HEADS, HEAD_DIM)
    values = qkv[:, 2 * D:].reshape(L, HEADS, HEAD_DIM)
    scores = jnp.einsum('qhe,khe->hqk', query, keys, precision=lax.Precision.HIGHEST) * HEAD_DIM ** (-0.5)
    scores = low_back(scores)
    allowed = id_row[:, None] == id_row[None, :]
    scores = jnp.where(allowed[None, :, :], scores, far_below)
    top = lax.optimization_barrier(jnp.max(scores, axis=-1, keepdims=True))
    expo = jnp.exp(scores - top)
    probs = expo / lax.optimization_barrier(jnp.sum(expo, axis=-1, keepdims=True))
    attended = jnp.einsum('hqk,khe->qhe', low(probs), values, precision=lax.Precision.HIGHEST).reshape(L, D)
    attended = low(low_back(attended))
    branch = low_back(matmul(attended, w_proj) + b_proj)
    mid = x_row + keep_attn[:, None] * branch
    h_two = low(layer_norm(mid, gain_two, bias_two))
    hidden = low_back(matmul(h_two, w_fc1) + b_fc1)
    gelled = low(jax.nn.gelu(hidden, approximate=False))
    mlp_out = low_back(matmul(gelled, w_fc2) + b_fc2)
    return mid + keep_mlp[:, None] * mlp_out

def reference(layer_input, out_grad, lengths, keep, ln1_gain, ln1_bias, w_qkv, b_query, b_value, w_proj, b_proj, ln2_gain, ln2_bias, w_fc1, b_fc1, w_fc2, b_fc2):
    image_id, keeps = token_tables(lengths, keep)
    valid = (image_id < IMGS).astype(jnp.float32)
    params = (ln1_gain.astype(jnp.float32), ln1_bias.astype(jnp.float32), w_qkv.astype(jnp.float32), b_query.astype(jnp.float32), b_value.astype(jnp.float32), w_proj.astype(jnp.float32), b_proj.astype(jnp.float32), ln2_gain.astype(jnp.float32), ln2_bias.astype(jnp.float32), w_fc1.astype(jnp.float32), b_fc1.astype(jnp.float32), w_fc2.astype(jnp.float32), b_fc2.astype(jnp.float32))

    def forward(x_float, *weights):

        def one_row(item):
            x_row, id_row, keep_attn, keep_mlp = item
            return row_layer(weights, x_row, id_row, keep_attn, keep_mlp)
        masked = x_float * valid[:, :, None]
        return lax.map(jax.checkpoint(one_row), (masked, image_id, keeps[0], keeps[1]))
    result, pull = jax.vjp(forward, layer_input.astype(jnp.float32), *params)
    grads = pull(out_grad.astype(jnp.float32))
    return (result.astype(jnp.bfloat16), grads[0].astype(jnp.bfloat16), grads[1], grads[2], grads[3], grads[4], grads[5], grads[6], grads[7], grads[8], grads[9], grads[10], grads[11], grads[12], grads[13])
```

```python
import math

import jax
import jax.numpy as jnp
from jax import lax
from jax.sharding import Mesh
from jax.sharding import PartitionSpec as P

D = 768
HEADS = 12
HEAD_DIM = 64
FF = 3072
IMGS = 4
TP = 8
COLS = D // TP
HID = FF // TP
PAIR = 2 * HEAD_DIM
VEC_ROWS = 16

eps_norm = 1e-06
drop_scale = 1.0 / 0.9
far_below = -1e30
inv_root_two = 1.0 / math.sqrt(2.0)
inv_root_tau = 1.0 / math.sqrt(2.0 * math.pi)

BLK = ("x", "yl")
bf16 = jnp.bfloat16
f32 = jnp.float32


def dot(a, b, dims):
    return lax.dot_general(a, b, ((dims[0], dims[1]), ((), ())), preferred_element_type=f32)


def normalize(values):
    mean = jnp.mean(values, axis=-1, keepdims=True)
    centred = values - mean
    inverse = lax.rsqrt(jnp.mean(centred * centred, axis=-1, keepdims=True) + eps_norm)
    return (centred * inverse, inverse)


def norm_back(grad_out, normed, inverse, gain):
    scaled = grad_out * gain
    inner = (
        scaled
        - jnp.mean(scaled, axis=-1, keepdims=True)
        - normed * jnp.mean(scaled * normed, axis=-1, keepdims=True)
    )
    return (inverse * inner, jnp.sum(grad_out * normed, axis=0), jnp.sum(grad_out, axis=0))


def spread(block, axes, count):
    tiled = jnp.broadcast_to(block[None], (count,) + block.shape)
    return lax.all_to_all(tiled, axes, 0, 0)


def exchange(block, axis, by_core):
    sizes = [2 if name in ("c", "yh", "yl") else 4 for name in axis]
    route = []
    for place in range(math.prod(sizes)):
        left, spots = place, {}
        for name, size in reversed(list(zip(axis, sizes))):
            left, spots[name] = divmod(left, size)
        mask = by_core[spots["c"]]
        if "yh" in spots:
            spots["yh"] ^= mask // 2
            spots["yl"] ^= mask % 2
        else:
            spots[axis[0] if axis[0] != "c" else axis[1]] ^= mask
        partner = 0
        for name, size in zip(axis, sizes):
            partner = partner * size + spots[name]
        route.append((place, partner))
    return lax.ppermute(block, axis, route)


def swap_core(block):
    return lax.ppermute(block, "c", [(0, 1), (1, 0)])


def sum_rows(partial, extra):
    core = lax.axis_index("c")
    halves = partial.reshape(2, HID, HID)
    mine = lax.dynamic_index_in_dim(halves, core, 0, keepdims=False)
    other = lax.dynamic_index_in_dim(halves, 1 - core, 0, keepdims=False)
    if extra is not None:
        mine = jnp.concatenate([mine, extra], axis=0)
        other = jnp.concatenate([other, extra], axis=0)
    got = swap_core(other.astype(bf16))
    half = (mine + got.astype(f32)).astype(bf16)
    pieces = half[:HID].reshape(8, HID // 8, HID)
    if extra is not None:
        tail = jnp.broadcast_to(half[HID:][None], (8, VEC_ROWS, HID))
        pieces = jnp.concatenate([pieces, tail], axis=1)
    pieces = lax.all_to_all(pieces, ("yh", "z"), 0, 0)
    return jnp.sum(pieces.astype(f32), axis=0).astype(bf16)


def double_twice(block, axis):
    one = exchange(block, axis, (1, 3))
    block = jnp.stack([block, one])
    two = exchange(block, axis, (3, 1))
    return jnp.concatenate([block, two])


def in_order(relative, place):
    core = lax.axis_index("c")
    first = jnp.array([0, 1, 3, 2], jnp.int32)
    second = jnp.array([0, 2, 3, 1], jnp.int32)
    table = jnp.where(core == 0, first, second)
    spots = [table[place ^ v] for v in range(4)]
    return jnp.stack([lax.dynamic_index_in_dim(relative, s, 0, keepdims=False) for s in spots])


def both_cores(block):
    core = lax.axis_index("c")
    got = swap_core(block)
    return jnp.stack([jnp.where(core == 0, block, got), jnp.where(core == 0, got, block)])


def per_device(
    layer_input,
    out_grad,
    lengths,
    keep,
    ln1_gain,
    ln1_bias,
    w_qkv,
    b_query,
    b_value,
    w_proj,
    b_proj,
    ln2_gain,
    ln2_bias,
    w_fc1,
    b_fc1,
    w_fc2,
    b_fc2,
):
    _, tokens, width = layer_input.shape
    row = tokens * TP
    group = lax.axis_index(BLK)
    ends = jnp.cumsum(lengths[0])
    places = jnp.arange(row, dtype=jnp.int32)
    ids = jnp.sum((ends[:, None] <= places[None, :]).astype(jnp.int32), axis=0)
    valid = (ids < IMGS).astype(f32)
    onehot = (ids[:, None] == jnp.arange(IMGS, dtype=jnp.int32)[None, :]).astype(f32)
    keeps = jnp.sum(onehot[None] * keep[:, 0, None, :].astype(f32), axis=2) * drop_scale
    here = group * tokens

    def own(v):
        return lax.dynamic_slice_in_dim(v, here, tokens, 0)

    own_ids = own(ids)
    scale_attn = own(keeps[0])[:, None]
    scale_mlp = own(keeps[1])[:, None]
    qkv_bias = jnp.concatenate([b_query, jnp.zeros_like(b_query), b_value])

    x_all = spread(layer_input[0], BLK, TP).reshape(row, width).astype(f32) * valid[:, None]
    normed_all, _ = normalize(x_all)
    h_all = (normed_all * ln1_gain + ln1_bias).astype(bf16)
    x_own = layer_input[0].astype(f32) * own(valid)[:, None]
    normed_one, inverse_one = normalize(x_own)
    h_own = (normed_one * ln1_gain + ln1_bias).astype(bf16)
    grad_z = out_grad[0].astype(f32)
    grad_mlp = (scale_mlp * grad_z).astype(bf16)
    grad_mlp_all = spread(grad_mlp, BLK, TP).reshape(row, width)

    query = (dot(h_own, w_qkv[:, :width], ((1,), (0,))) + b_query).astype(bf16)
    pairs = (dot(h_all, w_qkv[:, width:], ((1,), (0,))) + qkv_bias[width:]).astype(bf16)
    query = query.reshape(tokens, HEADS, HEAD_DIM)
    keys = pairs[:, :width].reshape(row, HEADS, HEAD_DIM)
    values = pairs[:, width:].reshape(row, HEADS, HEAD_DIM)
    scores = jnp.einsum("qhe,khe->hqk", query, keys, preferred_element_type=f32) * HEAD_DIM**-0.5
    allowed = own_ids[:, None] == ids[None, :]
    scores = jnp.where(allowed[None], scores, far_below)
    top = jnp.max(scores, axis=-1, keepdims=True)
    expo = jnp.exp(scores - top)
    probs = (expo / jnp.sum(expo, axis=-1, keepdims=True)).astype(bf16)
    attended = jnp.einsum("hqk,khe->qhe", probs, values, preferred_element_type=f32)
    attended = attended.reshape(tokens, width).astype(bf16)
    attended_all = spread(attended, BLK, TP).reshape(row, width)

    branch = dot(attended, w_proj, ((1,), (0,))) + b_proj
    mid = x_own + scale_attn * branch
    normed_two, inverse_two = normalize(mid)
    h_two = (normed_two * ln2_gain + ln2_bias).astype(bf16)
    hidden = dot(h_two, w_fc1, ((1,), (0,))) + b_fc1
    cumulative = 0.5 * (1.0 + lax.erf(hidden * inv_root_two))
    density = jnp.exp(-0.5 * hidden * hidden) * inv_root_tau
    gelled = (hidden * cumulative).astype(bf16)
    mlp_out = dot(gelled, w_fc2, ((1,), (0,))) + b_fc2
    output = (mid + scale_mlp * mlp_out).astype(bf16)
    grad_gelled = dot(grad_mlp, w_fc2, ((1,), (1,)))
    grad_hidden = (grad_gelled * (cumulative + hidden * density)).astype(bf16)
    grad_h_two = dot(grad_hidden, w_fc1, ((1,), (1,)))
    grad_mid_norm, ln2_gain_sum, ln2_bias_sum = norm_back(
        grad_h_two, normed_two, inverse_two, ln2_gain
    )
    grad_mid = grad_z + grad_mid_norm
    grad_branch = (scale_attn * grad_mid).astype(bf16)
    grad_att = dot(grad_branch, w_proj, ((1,), (1,))).astype(bf16)
    b_fc2_sum = jnp.sum(grad_mlp.astype(f32), axis=0)

    def first_head(j):
        return 3 * (j // 2) + j % 2

    outgoing = jnp.stack(
        [
            jnp.concatenate(
                [
                    grad_att[:, first_head(j) * HEAD_DIM :][:, :PAIR],
                    grad_branch[:, j * COLS : (j + 1) * COLS],
                    jnp.zeros((tokens, 2 * PAIR - PAIR - COLS), bf16),
                ],
                axis=1,
            )
            for j in range(TP)
        ]
    )
    incoming = lax.all_to_all(outgoing, BLK, 0, 0).reshape(row, 2 * PAIR)
    grad_att_pair = incoming[:, :PAIR]
    grad_branch_cols = incoming[:, PAIR : PAIR + COLS]

    start = first_head(group) * HEAD_DIM
    shift = (group % 2) * (HEAD_DIM // 2)
    w_pair = [
        lax.dynamic_slice(w_qkv, (0, t * width + start), (width, PAIR)) for t in range(3)
    ]
    bias_pair = [
        lax.dynamic_slice_in_dim(b_query, start, PAIR, 0),
        jnp.zeros((PAIR,), f32),
        lax.dynamic_slice_in_dim(b_value, start, PAIR, 0),
    ]
    qkv_pair = [
        (dot(h_all, w, ((1,), (0,))) + b).astype(bf16).reshape(row, 2, HEAD_DIM)
        for w, b in zip(w_pair, bias_pair)
    ]
    q2, k2, v2 = qkv_pair
    scores2 = jnp.einsum("qhe,khe->hqk", q2, k2, preferred_element_type=f32) * HEAD_DIM**-0.5
    allowed2 = ids[:, None] == ids[None, :]
    scores2 = jnp.where(allowed2[None], scores2, far_below)
    expo2 = jnp.exp(scores2 - jnp.max(scores2, axis=-1, keepdims=True))
    probs2 = expo2 / jnp.sum(expo2, axis=-1, keepdims=True)
    dob = grad_att_pair.reshape(row, 2, HEAD_DIM)
    dp2 = jnp.einsum("qhe,khe->hqk", dob, v2, preferred_element_type=f32)
    delta = jnp.sum(probs2 * dp2, axis=-1, keepdims=True)
    ds = (probs2 * (dp2 - delta)).astype(bf16)
    dq = jnp.einsum("hqk,khe->qhe", ds, k2, preferred_element_type=f32) * HEAD_DIM**-0.5
    dk = jnp.einsum("hqk,qhe->khe", ds, q2, preferred_element_type=f32) * HEAD_DIM**-0.5
    dv = jnp.einsum("hqk,qhe->khe", probs2.astype(bf16), dob, preferred_element_type=f32)
    parts = [
        lax.dynamic_slice(t.reshape(row, PAIR), (0, shift), (row, COLS)).astype(bf16)
        for t in (dq, dk, dv)
    ]
    dqkv = jnp.concatenate(parts, axis=1)
    dqkv_own = lax.all_to_all(dqkv.reshape(TP, tokens, 3 * COLS), BLK, 0, 0)
    w_cols = jnp.concatenate(
        [lax.dynamic_slice(w, (0, shift), (width, COLS)) for w in w_pair], axis=1
    )
    grad_h_cols = dot(dqkv, w_cols, ((1,), (1,)))
    ln1_gain_sum = jnp.sum(grad_h_cols * normed_all, axis=0)
    ln1_bias_sum = jnp.sum(grad_h_cols, axis=0)
    grad_b = jnp.concatenate(
        [dot(dqkv, h_all, ((0,), (0,))), dot(grad_branch_cols, attended_all, ((0,), (0,)))]
    )
    dqkv_sums = jnp.sum(dqkv.astype(f32), axis=0)
    b_proj_sum = jnp.sum(grad_branch_cols.astype(f32), axis=0)

    branch_all = dot(attended_all, w_proj, ((1,), (0,))) + b_proj
    mid_all = x_all + keeps[0][:, None] * branch_all
    h_two_all = (normalize(mid_all)[0] * ln2_gain + ln2_bias).astype(bf16)
    w_one = lax.dynamic_slice_in_dim(w_fc1, group * HID, HID, 1)
    w_two = lax.dynamic_slice_in_dim(w_fc2, group * HID, HID, 0)
    hid = dot(h_two_all, w_one, ((1,), (0,))) + lax.dynamic_slice_in_dim(b_fc1, group * HID, HID, 0)
    cumul = 0.5 * (1.0 + lax.erf(hid * inv_root_two))
    dens = jnp.exp(-0.5 * hid * hid) * inv_root_tau
    gel = (hid * cumul).astype(bf16)
    grad_hid = (dot(grad_mlp_all, w_two, ((1,), (1,))) * (cumul + hid * dens)).astype(bf16)
    grad_one = dot(h_two_all, grad_hid, ((0,), (0,)))
    grad_two = dot(gel, grad_mlp_all, ((0,), (0,)))
    b_fc1_sum = jnp.sum(grad_hid.astype(f32), axis=0)

    dqkv_rows = jnp.transpose(dqkv_own.reshape(TP, tokens, 3, COLS), (1, 2, 0, 3))
    grad_h_one = dot(dqkv_rows.reshape(tokens, 3 * width), w_qkv, ((1,), (1,)))
    grad_x_norm, _, _ = norm_back(grad_h_one, normed_one, inverse_one, ln1_gain)
    x_grad = ((grad_mid + grad_x_norm) * own(valid)[:, None]).astype(bf16)

    vec = jnp.concatenate(
        [
            ln1_gain_sum,
            ln1_bias_sum,
            ln2_gain_sum,
            ln2_bias_sum,
            b_fc2_sum,
            b_fc1_sum,
            dqkv_sums[:COLS],
            dqkv_sums[2 * COLS :],
            b_proj_sum,
            jnp.zeros((VEC_ROWS * HID - 11 * HID - 3 * COLS,), f32),
        ]
    ).reshape(VEC_ROWS, HID)

    def halves(m):
        return jnp.concatenate([m[:, :HID], m[:, HID:]], axis=0)

    piece_one = sum_rows(grad_one, None)
    piece_two = sum_rows(halves(grad_two), None)
    piece_b = sum_rows(halves(grad_b), vec)
    early_one = spread(piece_one, ("yh", "z", "yl"), 16)
    early_two = spread(piece_two, ("z", "x"), 16)
    early_b = spread(piece_b, ("yh", "x", "yl"), 16)
    vec_all = early_b.reshape(2, TP, HID // 8 + VEC_ROWS, HID)[0, :, HID // 8 :].astype(f32)
    early_b = early_b[:, : HID // 8]
    axis_x = ("c", "x")
    axis_y = ("yh", "c", "yl")
    axis_z = ("z", "c")
    whole_one = in_order(double_twice(early_one, axis_x), lax.axis_index("x"))
    whole_two = in_order(double_twice(early_two, axis_y), lax.axis_index(("yh", "yl")))
    whole_b = in_order(double_twice(early_b, axis_z), lax.axis_index("z"))
    one = both_cores(whole_one).reshape(2, 4, 2, 4, 2, HID // 8, HID)
    grad_w_fc1 = jnp.transpose(one, (0, 2, 3, 5, 1, 4, 6)).reshape(D, FF).astype(f32)
    two = both_cores(whole_two).reshape(2, 2, 2, 4, 4, HID // 8, HID)
    grad_w_fc2 = jnp.transpose(two, (4, 2, 1, 3, 5, 0, 6)).reshape(FF, D).astype(f32)
    b = both_cores(whole_b).reshape(2, 4, 2, TP, HID // 8, HID)
    b = jnp.transpose(b, (0, 5, 2, 1, 3, 4)).reshape(D, 4, 2, TP, HID // 8)
    b = jnp.transpose(b, (0, 1, 3, 2, 4)).reshape(D, 4 * D).astype(f32)
    flat = vec_all.reshape(TP, VEC_ROWS * HID)
    shared = jnp.sum(flat[:, : 5 * D], axis=0).reshape(5, D)
    tail = flat[:, 5 * D + HID :]
    return (
        output[None],
        x_grad[None],
        shared[0],
        shared[1],
        b[:, : 3 * D],
        tail[:, :COLS].reshape(D),
        tail[:, COLS : 2 * COLS].reshape(D),
        b[:, 3 * D :],
        tail[:, 2 * COLS : 3 * COLS].reshape(D),
        shared[2],
        shared[3],
        grad_w_fc1,
        flat[:, 5 * D : 5 * D + HID].reshape(FF),
        grad_w_fc2,
        shared[4],
    )


def solution(mesh):
    fine = Mesh(mesh.devices.reshape(2, 4, 2, 4, 2), ("yh", "z", "c", "x", "yl"))
    dp = ("yh", "z", "c")
    tokens = P(dp, BLK, None)
    placed = (tokens, tokens, P(dp, None), P(None, dp, None)) + (P(),) * 13
    return jax.shard_map(
        per_device,
        mesh=fine,
        in_specs=placed,
        out_specs=(tokens, tokens) + (P(),) * 13,
        check_vma=False,
    )
```

```python
import math

import jax
import jax.numpy as jnp
from jax import lax
from jax.experimental import pallas as pl
from jax.experimental.pallas import tpu as pltpu
from jax.sharding import Mesh
from jax.sharding import PartitionSpec as P

D = 768
HEADS = 12
HEAD_DIM = 64
FF = 3072
IMGS = 4
TP = 8
COLS = D // TP
HID = FF // TP
PAIR = 2 * HEAD_DIM
VEC_ROWS = 16
PIECE = (2 * TP, HID // TP, HID)

eps_norm = 1e-06
drop_scale = 1.0 / 0.9
far_below = -1e30
inv_root_two = 1.0 / math.sqrt(2.0)
inv_root_tau = 1.0 / math.sqrt(2.0 * math.pi)

BLK = ("x", "yl")
bf16 = jnp.bfloat16
f32 = jnp.float32


def dot(a, b, dims):
    return lax.dot_general(a, b, ((dims[0], dims[1]), ((), ())), preferred_element_type=f32)


def normalize(values):
    mean = jnp.mean(values, axis=-1, keepdims=True)
    centred = values - mean
    inverse = lax.rsqrt(jnp.mean(centred * centred, axis=-1, keepdims=True) + eps_norm)
    return (centred * inverse, inverse)


def norm_back(grad_out, normed, inverse, gain):
    scaled = grad_out * gain
    inner = (
        scaled
        - jnp.mean(scaled, axis=-1, keepdims=True)
        - normed * jnp.mean(scaled * normed, axis=-1, keepdims=True)
    )
    return (inverse * inner, jnp.sum(grad_out * normed, axis=0), jnp.sum(grad_out, axis=0))


def spread(block, axes, count):
    tiled = jnp.broadcast_to(block[None], (count,) + block.shape)
    return lax.all_to_all(tiled, axes, 0, 0)


def exchange(block, axis, by_core):
    sizes = [2 if name in ("c", "yh", "yl") else 4 for name in axis]
    route = []
    for place in range(math.prod(sizes)):
        left, spots = place, {}
        for name, size in reversed(list(zip(axis, sizes))):
            left, spots[name] = divmod(left, size)
        mask = by_core[spots["c"]]
        if "yh" in spots:
            spots["yh"] ^= mask // 2
            spots["yl"] ^= mask % 2
        else:
            spots[axis[0] if axis[0] != "c" else axis[1]] ^= mask
        partner = 0
        for name, size in zip(axis, sizes):
            partner = partner * size + spots[name]
        route.append((place, partner))
    return lax.ppermute(block, axis, route)


def swap_core(block):
    return lax.ppermute(block, "c", [(0, 1), (1, 0)])


def sum_rows(partial, extra):
    core = lax.axis_index("c")
    halves = partial.reshape(2, HID, HID)
    mine = lax.dynamic_index_in_dim(halves, core, 0, keepdims=False)
    other = lax.dynamic_index_in_dim(halves, 1 - core, 0, keepdims=False)
    if extra is not None:
        mine = jnp.concatenate([mine, extra], axis=0)
        other = jnp.concatenate([other, extra], axis=0)
    got = swap_core(other.astype(bf16))
    half = (mine + got.astype(f32)).astype(bf16)
    pieces = half[:HID].reshape(8, HID // 8, HID)
    if extra is not None:
        tail = jnp.broadcast_to(half[HID:][None], (8, VEC_ROWS, HID))
        pieces = jnp.concatenate([pieces, tail], axis=1)
    pieces = lax.all_to_all(pieces, ("yh", "z"), 0, 0)
    return jnp.sum(pieces.astype(f32), axis=0).astype(bf16)


def whole(shape):
    return pl.BlockSpec(shape, lambda *_: (0,) * len(shape))


def column(v):
    return v.reshape(-1, 1)


def line(v):
    return v.reshape(1, -1)


def gelu_parts(u):
    cumulative = 0.5 * (1.0 + lax.erf(u * inv_root_two))
    density = jnp.exp(-0.5 * u * u) * inv_root_tau
    return (u * cumulative, cumulative + u * density)


def launch(body, grid, scalars, ins, outs, scratch, flops, moved):
    arrays = [a for a, _ in ins]
    return pl.pallas_call(
        body,
        grid_spec=pltpu.PrefetchScalarGridSpec(
            num_scalar_prefetch=1,
            grid=grid,
            in_specs=[spec for _, spec in ins],
            out_specs=[spec for _, spec in outs],
            scratch_shapes=scratch,
        ),
        out_shape=[shape for shape, _ in outs],
        compiler_params=pltpu.CompilerParams(vmem_limit_bytes=56 * 1024 * 1024),
        cost_estimate=pl.CostEstimate(flops=flops, bytes_accessed=moved, transcendentals=0),
    )(scalars, *arrays)


def shaped(shape, dtype):
    return jax.ShapeDtypeStruct(shape, dtype)


def attend_kernel(
    at, x, ids_col, ids_row, gain, bias, wq, wk, wv, bq, bv, out, h_all, xhat_all, block
):
    row = x.shape[0]
    tokens = out.shape[0]
    here = pl.multiple_of(at[0], tokens)

    @pl.when(pl.program_id(0) == 0)
    def _():
        def norm(i, _):
            spot = pl.ds(pl.multiple_of(i * tokens, tokens), tokens)
            valid = (ids_col[spot] < IMGS).astype(f32)
            normed, _inverse = normalize(x[spot].astype(f32) * valid)
            xhat_all[spot] = normed.astype(bf16)
            h_all[spot] = (normed * gain[...] + bias[...]).astype(bf16)
            return 0

        lax.fori_loop(0, row // tokens, norm, 0)
        mine = ids_col[pl.ds(here, tokens)]
        block[...] = jnp.where(mine == ids_row[...], 0.0, far_below)

    h = h_all[...]
    keys = dot(h, wk[...], ((1,), (0,))).astype(bf16)
    values = (dot(h, wv[...], ((1,), (0,))) + bv[...]).astype(bf16)
    query = dot(h_all[pl.ds(here, tokens)], wq[...], ((1,), (0,))) + bq[...]
    low = lax.broadcasted_iota(jnp.int32, (tokens, PAIR), 1) < HEAD_DIM
    both = jnp.concatenate([jnp.where(low, query, 0.0), jnp.where(low, 0.0, query)])
    scores = dot(both.astype(bf16), keys, ((1,), (1,))) * HEAD_DIM**-0.5
    scores = scores.reshape(2, tokens, row) + block[...][None]
    scores = scores.reshape(2 * tokens, row)
    expo = jnp.exp(scores - jnp.max(scores, axis=-1, keepdims=True))
    probs = (expo * (1.0 / jnp.sum(expo, axis=-1, keepdims=True))).astype(bf16)
    result = dot(probs, values, ((1,), (0,)))
    out[...] = jnp.where(low, result[:tokens], result[tokens:]).astype(bf16)


def attend(at, x_all, ids, gain, bias, w_qkv, b_query, b_value, tokens):
    row, width = x_all.shape
    steps = width // PAIR
    part = pl.BlockSpec((width, PAIR), lambda p, _: (0, p))
    part_k = pl.BlockSpec((width, PAIR), lambda p, _: (0, steps + p))
    part_v = pl.BlockSpec((width, PAIR), lambda p, _: (0, 2 * steps + p))
    small = pl.BlockSpec((1, PAIR), lambda p, _: (0, p))
    return launch(
        attend_kernel,
        (steps,),
        at,
        [
            (x_all, whole((row, width))),
            (column(ids), whole((row, 1))),
            (line(ids), whole((1, row))),
            (line(gain), whole((1, width))),
            (line(bias), whole((1, width))),
            (w_qkv, part),
            (w_qkv, part_k),
            (w_qkv, part_v),
            (line(b_query), small),
            (line(b_value), small),
        ],
        [
            (shaped((tokens, width), bf16), pl.BlockSpec((tokens, PAIR), lambda p, _: (0, p))),
            (shaped((row, width), bf16), whole((row, width))),
            (shaped((row, width), bf16), whole((row, width))),
        ],
        [pltpu.VMEM((tokens, row), f32)],
        6 * 10**9,
        10**7,
    )


def first_head(j):
    return 3 * (j // 2) + j % 2


def mlp_kernel(
    _,
    att,
    x,
    marks,
    grad_z,
    w_proj,
    b_proj,
    gain,
    bias,
    w_one,
    b_one,
    w_two,
    b_two,
    out,
    grad_mid,
    outgoing,
    sums,
    mid,
    normed,
    inverse,
    h_two,
    grad_mlp,
    total,
    grad_h,
):
    step = pl.program_id(0)
    scale_attn, scale_mlp = marks[:, 0:1], marks[:, 1:2]

    @pl.when(step == 0)
    def _():
        branch = dot(att[...], w_proj[...], ((1,), (0,))) + b_proj[...]
        y = x[...].astype(f32) * marks[:, 2:3] + scale_attn * branch
        mid[...] = y
        hat, inv = normalize(y)
        normed[...] = hat
        inverse[...] = inv
        h_two[...] = (hat * gain[...] + bias[...]).astype(bf16)
        grad_mlp[...] = (scale_mlp * grad_z[...].astype(f32)).astype(bf16)
        total[...] = jnp.zeros_like(total)
        grad_h[...] = jnp.zeros_like(grad_h)

    hidden = dot(h_two[...], w_one[...], ((1,), (0,))) + b_one[...]
    gelled, slope = gelu_parts(hidden)
    total[...] += dot(gelled.astype(bf16), w_two[...], ((1,), (0,)))
    grad_hidden = (dot(grad_mlp[...], w_two[...], ((1,), (1,))) * slope).astype(bf16)
    grad_h[...] += dot(grad_hidden, w_one[...], ((1,), (1,)))

    @pl.when(step == pl.num_programs(0) - 1)
    def _():
        out[...] = (mid[...] + scale_mlp * (total[...] + b_two[...])).astype(bf16)
        back, gain_sum, bias_sum = norm_back(grad_h[...], normed[...], inverse[...], gain[...])
        grad_y = grad_z[...].astype(f32) + back
        grad_mid[...] = grad_y
        sums[0:1] = line(gain_sum)
        sums[1:2] = line(bias_sum)
        sums[2:3] = line(jnp.sum(grad_mlp[...].astype(f32), axis=0))
        sums[3:8] = jnp.zeros((5, sums.shape[1]), f32)
        branch_t = jnp.transpose(scale_attn * grad_y).astype(bf16)
        att_t = dot(w_proj[...], branch_t, ((1,), (0,))).astype(bf16)
        for j in range(TP):
            start = first_head(j) * HEAD_DIM
            outgoing[j, :PAIR] = att_t[start : start + PAIR]
            outgoing[j, PAIR:] = branch_t[j * COLS : (j + 1) * COLS]


def mlp(att, x, marks, grad_z, w_proj, b_proj, gain, bias, w_one, b_one, w_two, b_two):
    tokens, width = x.shape
    chunk = 512
    tw = whole((tokens, width))
    return launch(
        mlp_kernel,
        (FF // chunk,),
        jnp.zeros((1,), jnp.int32),
        [
            (att, tw),
            (x, tw),
            (marks, whole(marks.shape)),
            (grad_z, tw),
            (w_proj, whole((width, width))),
            (line(b_proj), whole((1, width))),
            (line(gain), whole((1, width))),
            (line(bias), whole((1, width))),
            (w_one, pl.BlockSpec((width, chunk), lambda p, _: (0, p))),
            (line(b_one), pl.BlockSpec((1, chunk), lambda p, _: (0, p))),
            (w_two, pl.BlockSpec((chunk, width), lambda p, _: (p, 0))),
            (line(b_two), whole((1, width))),
        ],
        [
            (shaped((tokens, width), bf16), tw),
            (shaped((tokens, width), f32), tw),
            (shaped((TP, PAIR + COLS, tokens), bf16), whole((TP, PAIR + COLS, tokens))),
            (shaped((8, width), f32), whole((8, width))),
        ],
        [
            pltpu.VMEM((tokens, width), f32),
            pltpu.VMEM((tokens, width), f32),
            pltpu.VMEM((tokens, 1), f32),
            pltpu.VMEM((tokens, width), bf16),
            pltpu.VMEM((tokens, width), bf16),
            pltpu.VMEM((tokens, width), f32),
            pltpu.VMEM((tokens, width), f32),
        ],
        3 * 10**9,
        11 * 10**6,
    )


def pair_kernel(_, h, w, b, ids_col, ids_row, query, key_t, value, probs, att_t, keys, value_t):
    block = probs.shape[2]

    @pl.when(pl.program_id(0) == 0)
    def _():
        def make(i, _):
            spot = pl.ds(pl.multiple_of(i * block, block), block)
            qkv = dot(h[spot], w[...], ((1,), (0,))) + b[...]
            query[spot] = qkv[:, :PAIR].astype(bf16)
            keys[spot] = qkv[:, PAIR : 2 * PAIR].astype(bf16)
            value[spot] = qkv[:, 2 * PAIR :].astype(bf16)
            key_t[:, spot] = jnp.transpose(qkv[:, PAIR : 2 * PAIR]).astype(bf16)
            value_t[:, spot] = jnp.transpose(qkv[:, 2 * PAIR :]).astype(bf16)
            return 0

        lax.fori_loop(0, h.shape[0] // block, make, 0)

    here = pl.ds(pl.multiple_of(pl.program_id(0) * block, block), block)
    allowed = ids_col[...] == ids_row[...]
    k = keys[...]
    low = lax.broadcasted_iota(jnp.int32, k.shape, 1) < HEAD_DIM
    for e in range(2):
        k_e = jnp.where(low == (e == 0), k, jnp.zeros_like(k))
        scores = dot(k_e, query[here], ((1,), (1,))) * HEAD_DIM**-0.5
        scores = jnp.where(allowed, scores, far_below)
        expo = jnp.exp(scores - jnp.max(scores, axis=0, keepdims=True))
        p = (expo * (1.0 / jnp.sum(expo, axis=0, keepdims=True))).astype(bf16)
        probs[e] = p
        rows = slice(e * HEAD_DIM, (e + 1) * HEAD_DIM)
        att_t[rows] = dot(value_t[rows], p, ((1,), (0,)))


def pair_forward(h_all, w, b, ids):
    row, width = h_all.shape
    block = 256
    return launch(
        pair_kernel,
        (row // block,),
        jnp.zeros((1,), jnp.int32),
        [
            (h_all, whole((row, width))),
            (w, whole(w.shape)),
            (line(b), whole((1, 3 * PAIR))),
            (column(ids), whole((row, 1))),
            (line(ids), pl.BlockSpec((1, block), lambda i, _: (0, i))),
        ],
        [
            (shaped((row, PAIR), bf16), whole((row, PAIR))),
            (shaped((PAIR, row), bf16), whole((PAIR, row))),
            (shaped((row, PAIR), bf16), whole((row, PAIR))),
            (shaped((2, row, row), bf16), pl.BlockSpec((2, row, block), lambda i, _: (0, 0, i))),
            (shaped((PAIR, row), f32), pl.BlockSpec((PAIR, block), lambda i, _: (0, i))),
        ],
        [pltpu.VMEM((row, PAIR), bf16), pltpu.VMEM((PAIR, row), bf16)],
        3 * 10**9,
        8 * 10**6,
    )


def pair_back_kernel(
    shift,
    incoming,
    query,
    key_t,
    value,
    probs,
    att_t,
    h,
    xhat,
    w_t,
    grad_b,
    outgoing,
    sums,
    col_sums,
    grad_t,
    grad_rows,
    delta,
    d_t,
    d_key,
    d_value,
    flat,
):
    step = pl.program_id(0)
    tokens = incoming.shape[2]
    block = value.shape[0]

    @pl.when(step == 0)
    def _():
        for t in range(TP):
            spot = slice(t * tokens, (t + 1) * tokens)
            piece = incoming[t, :PAIR]
            grad_t[:, spot] = piece
            grad_rows[spot] = jnp.transpose(piece.astype(f32)).astype(bf16)
        prod = grad_t[...].astype(f32) * att_t[...]
        delta[0:1] = jnp.sum(prod[:HEAD_DIM], axis=0, keepdims=True)
        delta[1:2] = jnp.sum(prod[HEAD_DIM:], axis=0, keepdims=True)
        d_t[0] = jnp.zeros(d_t.shape[1:], f32)

    v = value[...]
    low = lax.broadcasted_iota(jnp.int32, v.shape, 1) < HEAD_DIM
    here = pl.ds(pl.multiple_of(step * block, block), block)
    dk, dv = [], []
    for e in range(2):
        v_e = jnp.where(low == (e == 0), v, jnp.zeros_like(v))
        p = probs[e]
        dp = dot(v_e, grad_t[...], ((1,), (0,)))
        ds = (p.astype(f32) * (dp - delta[e : e + 1])).astype(bf16)
        dk.append(dot(ds, query[...], ((1,), (0,))))
        dv.append(dot(p, grad_rows[...], ((1,), (0,))))
        rows = slice(e * HEAD_DIM, (e + 1) * HEAD_DIM)
        d_t[0, rows] += dot(key_t[rows, here], ds, ((1,), (0,)))
    d_key[here] = jnp.where(low, dk[0], dk[1])
    d_value[here] = jnp.where(low, dv[0], dv[1])

    @pl.when(step == pl.num_programs(0) - 1)
    def _():
        scale = HEAD_DIM**-0.5
        d_t[0] = d_t[0] * scale
        d_t[1] = jnp.transpose(d_key[...]) * scale
        d_t[2] = jnp.transpose(d_value[...])
        spot = pl.ds(pl.multiple_of(shift[0], HEAD_DIM // 2), COLS)
        gain_sum = jnp.zeros((1, h.shape[1]), f32)
        bias_sum = jnp.zeros((1, h.shape[1]), f32)
        for t in range(3):
            rows = slice(t * COLS, (t + 1) * COLS)
            part = d_t[t, spot].astype(bf16)
            flat[rows] = part
            s = jnp.sum(part.astype(f32), axis=1, keepdims=True)
            col_sums[rows] = s
            grad_b[rows] = dot(part, h[...], ((1,), (0,)))
            w = w_t[pl.ds(pl.multiple_of(t * PAIR + shift[0], HEAD_DIM // 2), COLS)].astype(f32)
            inner = dot(part, xhat[...], ((1,), (0,)))
            gain_sum += jnp.sum(w * inner, axis=0, keepdims=True)
            bias_sum += jnp.sum(w * s, axis=0, keepdims=True)
        for t in range(TP):
            outgoing[t] = flat[:, t * tokens : (t + 1) * tokens]
        sums[0:1] = gain_sum
        sums[1:2] = bias_sum
        sums[2:8] = jnp.zeros((6, sums.shape[1]), f32)


def pair_back(shift, incoming, query, key_t, value, probs, att_t, h_all, xhat_all, w_t):
    row, width = h_all.shape
    tokens = incoming.shape[2]
    block = 256
    return launch(
        pair_back_kernel,
        (row // block,),
        shift,
        [
            (incoming, whole(incoming.shape)),
            (query, whole((row, PAIR))),
            (key_t, whole((PAIR, row))),
            (value, pl.BlockSpec((block, PAIR), lambda i, _: (i, 0))),
            (probs, pl.BlockSpec((2, block, row), lambda i, _: (0, i, 0))),
            (att_t, whole((PAIR, row))),
            (h_all, whole((row, width))),
            (xhat_all, whole((row, width))),
            (w_t, whole(w_t.shape)),
        ],
        [
            (shaped((3 * COLS, width), f32), whole((3 * COLS, width))),
            (shaped((TP, 3 * COLS, tokens), bf16), whole((TP, 3 * COLS, tokens))),
            (shaped((8, width), f32), whole((8, width))),
            (shaped((3 * COLS, 1), f32), whole((3 * COLS, 1))),
        ],
        [
            pltpu.VMEM((PAIR, row), bf16),
            pltpu.VMEM((row, PAIR), bf16),
            pltpu.VMEM((8, row), f32),
            pltpu.VMEM((3, PAIR, row), f32),
            pltpu.VMEM((row, PAIR), f32),
            pltpu.VMEM((row, PAIR), f32),
            pltpu.VMEM((3 * COLS, row), bf16),
        ],
        6 * 10**9,
        10**7,
    )


def hidden_kernel(
    _,
    att,
    x,
    marks,
    grad_mlp,
    incoming,
    w_proj,
    b_proj,
    gain,
    bias,
    w_one,
    b_one,
    w_two,
    grad_one,
    grad_two,
    grad_proj,
    one_sum,
    proj_sum,
):
    @pl.when(pl.program_id(0) == 0)
    def _():
        grad_one[...] = jnp.zeros_like(grad_one)
        grad_two[...] = jnp.zeros_like(grad_two)
        grad_proj[...] = jnp.zeros_like(grad_proj)
        one_sum[...] = jnp.zeros_like(one_sum)
        proj_sum[...] = jnp.zeros_like(proj_sum)

    branch = dot(att[...], w_proj[...], ((1,), (0,))) + b_proj[...]
    y = x[...].astype(f32) * marks[:, 2:3] + marks[:, 0:1] * branch
    h = (normalize(y)[0] * gain[...] + bias[...]).astype(bf16)
    hidden = dot(h, w_one[...], ((1,), (0,))) + b_one[...]
    gelled, slope = gelu_parts(hidden)
    grad_hidden = (dot(grad_mlp[...], w_two[...], ((1,), (1,))) * slope).astype(bf16)
    grad_one[...] += dot(h, grad_hidden, ((0,), (0,)))
    grad_two[...] += dot(gelled.astype(bf16), grad_mlp[...], ((0,), (0,)))
    one_sum[0:1] += jnp.sum(grad_hidden.astype(f32), axis=0, keepdims=True)
    for t in range(incoming.shape[0]):
        piece = incoming[t, PAIR:]
        tokens = piece.shape[1]
        grad_proj[...] += dot(piece, att[t * tokens : (t + 1) * tokens], ((1,), (0,)))
        proj_sum[...] += jnp.sum(piece.astype(f32), axis=1, keepdims=True)


def hidden_grads(group, att, x, marks, grad_mlp, incoming, w_proj, b_proj, gain, bias, w_one, b_one, w_two):
    row, width = x.shape
    tokens = incoming.shape[2]
    block = 256
    tall = pl.BlockSpec((block, width), lambda i, _: (i, 0))
    rows_in = PAIR + COLS
    return launch(
        hidden_kernel,
        (row // block,),
        group,
        [
            (att, tall),
            (x, tall),
            (marks, pl.BlockSpec((block, marks.shape[1]), lambda i, _: (i, 0))),
            (grad_mlp, tall),
            (incoming, pl.BlockSpec((block // tokens, rows_in, tokens), lambda i, _: (i, 0, 0))),
            (w_proj, whole((width, width))),
            (line(b_proj), whole((1, width))),
            (line(gain), whole((1, width))),
            (line(bias), whole((1, width))),
            (w_one, pl.BlockSpec((width, HID), lambda i, g: (0, g[0]))),
            (line(b_one), pl.BlockSpec((1, HID), lambda i, g: (0, g[0]))),
            (w_two, pl.BlockSpec((HID, width), lambda i, g: (g[0], 0))),
        ],
        [
            (shaped((width, HID), f32), whole((width, HID))),
            (shaped((HID, width), f32), whole((HID, width))),
            (shaped((COLS, width), f32), whole((COLS, width))),
            (shaped((8, HID), f32), whole((8, HID))),
            (shaped((COLS, 1), f32), whole((COLS, 1))),
        ],
        [],
        4 * 10**9,
        10**7,
    )


def input_kernel(_, incoming, w_qkv, x, marks, grad_mid, gain, out, flat):
    width = x.shape[1]
    for j in range(TP):
        for t in range(3):
            flat[t * width + j * COLS : t * width + (j + 1) * COLS] = incoming[
                j, t * COLS : (t + 1) * COLS
            ]
    grad_h = jnp.transpose(dot(w_qkv[...], flat[...], ((1,), (0,))))
    valid = marks[:, 2:3]
    normed, inverse = normalize(x[...].astype(f32) * valid)
    back, _gain_sum, _bias_sum = norm_back(grad_h, normed, inverse, gain[...])
    out[...] = ((grad_mid[...] + back) * valid).astype(bf16)


def input_grad(incoming, w_qkv, x, marks, grad_mid, gain):
    tokens, width = x.shape
    tw = whole((tokens, width))
    return launch(
        input_kernel,
        (1,),
        jnp.zeros((1,), jnp.int32),
        [
            (incoming, whole(incoming.shape)),
            (w_qkv, whole(w_qkv.shape)),
            (x, tw),
            (marks, whole(marks.shape)),
            (grad_mid, tw),
            (line(gain), whole((1, width))),
        ],
        [(shaped((tokens, width), bf16), tw)],
        [pltpu.VMEM((3 * width, tokens), bf16)],
        10**9,
        5 * 10**6,
    )[0]


def place_kernel(tasks, n_arrays, n_old, at, *refs):
    arrays = refs[:n_arrays]
    one, two, qkv, proj, raw, wide, split, tall, sem_in, sem_out = refs[n_arrays + n_old :]
    core = at[3]
    first, second = 1 + 2 * core, 3 - 2 * core

    def load(i):
        _, array, entry, _, _ = tasks[i]
        return pltpu.make_async_copy(arrays[array].at[entry], raw.at[i % 2], sem_in.at[i % 2])

    def store(i, begin):
        part, _, _, hop, swapped = tasks[i]
        slot = i % 2
        hops = (0, second if swapped else first, first if swapped else second, 2)
        spot = at[part] ^ hops[hop]
        rows = pl.ds(pl.multiple_of((1 - core if swapped else core) * HID, HID), HID)
        done = sem_out.at[slot]

        def go(source, target):
            copy = pltpu.make_async_copy(source, target, done)
            if begin:
                copy.start()
            else:
                copy.wait()

        columns = pl.ds(pl.multiple_of(spot * D, D), D)
        if part == 0:
            go(wide.at[slot], one.at[rows, columns])
        elif part == 1:
            go(split.at[slot], two.at[:, spot % 2, spot // 2, :, rows])
        else:

            @pl.when(spot < 3)
            def _():
                go(wide.at[slot], qkv.at[rows, columns])

            @pl.when(spot == 3)
            def _():
                go(wide.at[slot], proj.at[rows, :])

    load(0).start()
    for i in range(len(tasks)):
        part = tasks[i][0]
        slot = i % 2
        if i + 1 < len(tasks):
            load(i + 1).start()
        load(i).wait()
        if i >= 2:
            store(i - 2, False)
        high = PIECE[1]
        for a in range(PIECE[0]):
            piece = raw[slot, a].astype(f32)
            if part == 0:
                wide[slot, a // 2 * high : a // 2 * high + high, a % 2 * HID : a % 2 * HID + HID] = piece
            elif part == 1:
                split[slot, a % 4, a // 4 * high : a // 4 * high + high] = piece
            else:
                start = (a % TP) * COLS + a // TP * high
                tall[start : start + high] = piece
        if part == 2:
            wide[slot] = jnp.transpose(tall[...])
        store(i, True)
    for i in range(max(0, len(tasks) - 2), len(tasks)):
        store(i, False)


def place_pieces(at, pieces, old):
    tasks, arrays = [], []
    for part, mine, other, hops in pieces:
        for swapped, array in ((False, mine), (True, other)):
            for entry, hop in enumerate(hops):
                tasks.append((part, len(arrays), entry, hop, swapped))
            arrays.append(array)
    shapes = [
        shaped((D, FF), f32),
        shaped((4, 2, 2, HID // 2, D), f32),
        shaped((D, 3 * D), f32),
        shaped((D, D), f32),
    ]
    anywhere = pl.BlockSpec(memory_space=pl.ANY)
    n_old = len(old)

    def body(*refs):
        place_kernel(tasks, len(arrays), n_old, *refs)

    return pl.pallas_call(
        body,
        grid_spec=pltpu.PrefetchScalarGridSpec(
            num_scalar_prefetch=1,
            grid=(1,),
            in_specs=[anywhere] * (len(arrays) + n_old),
            out_specs=[anywhere] * 4,
            scratch_shapes=[
                pltpu.VMEM((2,) + PIECE, bf16),
                pltpu.VMEM((2, HID, D), f32),
                pltpu.VMEM((2, 4, HID // 2, HID), f32),
                pltpu.VMEM((D, HID), f32),
                pltpu.SemaphoreType.DMA((2,)),
                pltpu.SemaphoreType.DMA((2,)),
            ],
        ),
        out_shape=shapes,
        input_output_aliases={1 + len(arrays) + i: i for i in range(n_old)},
        compiler_params=pltpu.CompilerParams(vmem_limit_bytes=56 * 1024 * 1024),
        cost_estimate=pl.CostEstimate(
            flops=0, bytes_accessed=1800000 * len(tasks), transcendentals=0
        ),
    )(at, *arrays, *old)


def per_device(
    layer_input,
    out_grad,
    lengths,
    keep,
    ln1_gain,
    ln1_bias,
    w_qkv,
    b_query,
    b_value,
    w_proj,
    b_proj,
    ln2_gain,
    ln2_bias,
    w_fc1,
    b_fc1,
    w_fc2,
    b_fc2,
):
    _, tokens, width = layer_input.shape
    row = tokens * TP
    group = lax.axis_index(BLK)
    ends = jnp.cumsum(lengths[0])
    places = jnp.arange(row, dtype=jnp.int32)
    ids = jnp.sum((ends[:, None] <= places[None, :]).astype(jnp.int32), axis=0)
    valid = (ids < IMGS).astype(f32)
    onehot = (ids[:, None] == jnp.arange(IMGS, dtype=jnp.int32)[None, :]).astype(f32)
    keeps = jnp.sum(onehot[None] * keep[:, 0, None, :].astype(f32), axis=2) * drop_scale
    here = group * tokens

    def own(v):
        return lax.dynamic_slice_in_dim(v, here, tokens, 0)


    x_all = spread(layer_input[0], BLK, TP).reshape(row, width)
    marks_all = jnp.stack([keeps[0], keeps[1], valid], axis=1)
    marks = own(marks_all)
    grad_mlp = (marks[:, 1:2] * out_grad[0].astype(f32)).astype(bf16)
    grad_mlp_all = spread(grad_mlp, BLK, TP).reshape(row, width)
    start = first_head(group) * HEAD_DIM
    shift = (group % 2) * (HEAD_DIM // 2)
    w_pair = jnp.concatenate(
        [lax.dynamic_slice(w_qkv, (0, t * width + start), (width, PAIR)) for t in range(3)], axis=1
    )
    bias_pair = jnp.concatenate(
        [
            lax.dynamic_slice_in_dim(b_query, start, PAIR, 0),
            jnp.zeros((PAIR,), f32),
            lax.dynamic_slice_in_dim(b_value, start, PAIR, 0),
        ]
    )
    w_pair_t = jnp.transpose(w_pair)

    attended, h_all, xhat_all = attend(
        here[None], x_all, ids, ln1_gain, ln1_bias, w_qkv, b_query, b_value, tokens
    )
    attended_all = spread(attended, BLK, TP).reshape(row, width)
    output, grad_mid, outgoing, sums_two = mlp(
        attended,
        layer_input[0],
        marks,
        out_grad[0],
        w_proj,
        b_proj,
        ln2_gain,
        ln2_bias,
        w_fc1,
        b_fc1,
        w_fc2,
        b_fc2,
    )
    incoming = lax.all_to_all(outgoing, BLK, 0, 0)
    pair = pair_forward(h_all, w_pair, bias_pair, ids)
    grad_qkv, back_out, sums_one, col_sums = pair_back(
        shift[None], incoming, *pair, h_all, xhat_all, w_pair_t
    )
    back_in = lax.all_to_all(back_out, BLK, 0, 0)
    grad_one, grad_two, grad_proj, one_sum, proj_sum = hidden_grads(
        group[None],
        attended_all,
        x_all,
        marks_all,
        grad_mlp_all,
        incoming,
        w_proj,
        b_proj,
        ln2_gain,
        ln2_bias,
        w_fc1,
        b_fc1,
        w_fc2,
    )
    x_grad = input_grad(back_in, w_qkv, layer_input[0], marks, grad_mid, ln1_gain)
    grad_b = jnp.concatenate([grad_qkv, grad_proj])

    vec = jnp.concatenate(
        [
            sums_one[0],
            sums_one[1],
            sums_two[0],
            sums_two[1],
            sums_two[2],
            one_sum[0],
            col_sums[:COLS, 0],
            col_sums[2 * COLS :, 0],
            proj_sum[:, 0],
            jnp.zeros((VEC_ROWS * HID - 11 * HID - 3 * COLS,), f32),
        ]
    ).reshape(VEC_ROWS, HID)

    def halves(m):
        return jnp.concatenate([m[:, :HID], m[:, HID:]], axis=0)

    ordered_b = jnp.transpose(grad_b.reshape(4, 2, HID // 8, D), (1, 0, 2, 3)).reshape(HID, D)
    piece_one = sum_rows(grad_one, None)
    piece_two = sum_rows(halves(grad_two), None)
    piece_b = sum_rows(halves(ordered_b), vec)
    early_one = spread(piece_one, ("yh", "z", "yl"), 16)
    early_two = spread(piece_two, ("z", "x"), 16)
    early_b = spread(piece_b, ("yh", "x", "yl"), 16)
    vec_all = early_b.reshape(2, TP, HID // 8 + VEC_ROWS, HID)[0, :, HID // 8 :].astype(f32)
    early_b = early_b[:, : HID // 8]
    at = jnp.stack(
        [lax.axis_index("x"), lax.axis_index(("yh", "yl")), lax.axis_index("z"), lax.axis_index("c")]
    ).astype(jnp.int32)
    axes = (("c", "x"), ("yh", "c", "yl"), ("z", "c"))
    parts = (early_one, early_two, early_b)
    near = [exchange(p, axis, (1, 3)) for p, axis in zip(parts, axes)]
    both = [jnp.stack([p, n]) for p, n in zip(parts, near)]
    far = [exchange(b, axis, (3, 1)) for b, axis in zip(both, axes)]
    outs = ()
    for stage, hops in (([p[None] for p in parts], (0,)), ([n[None] for n in near], (1,)), (far, (2, 3))):
        outs = place_pieces(
            at, [(i, p, swap_core(p), hops) for i, p in enumerate(stage)], tuple(outs)
        )
    grad_w_fc1, grad_w_fc2, grad_w_qkv, grad_w_proj = outs
    flat = vec_all.reshape(TP, VEC_ROWS * HID)
    shared = jnp.sum(flat[:, : 5 * D], axis=0).reshape(5, D)
    tail = flat[:, 5 * D + HID :]
    return (
        output[None],
        x_grad[None],
        shared[0],
        shared[1],
        grad_w_qkv,
        tail[:, :COLS].reshape(D),
        tail[:, COLS : 2 * COLS].reshape(D),
        grad_w_proj,
        tail[:, 2 * COLS : 3 * COLS].reshape(D),
        shared[2],
        shared[3],
        grad_w_fc1,
        flat[:, 5 * D : 5 * D + HID].reshape(FF),
        grad_w_fc2.reshape(FF, D),
        shared[4],
    )


def solution(mesh):
    fine = Mesh(mesh.devices.reshape(2, 4, 2, 4, 2), ("yh", "z", "c", "x", "yl"))
    dp = ("yh", "z", "c")
    tokens = P(dp, BLK, None)
    placed = (tokens, tokens, P(dp, None), P(None, dp, None)) + (P(),) * 13
    return jax.shard_map(
        per_device,
        mesh=fine,
        in_specs=placed,
        out_specs=(tokens, tokens) + (P(),) * 13,
        check_vma=False,
    )
```

```python
import math

import jax
import jax.numpy as jnp
from jax import lax
from jax.experimental import pallas as pl
from jax.experimental.pallas import tpu as pltpu
from jax.sharding import Mesh
from jax.sharding import PartitionSpec as P

D = 768
HEADS = 12
HEAD_DIM = 64
FF = 3072
IMGS = 4
TP = 8
COLS = D // TP
HID = FF // TP
PAIR = 2 * HEAD_DIM
VEC_ROWS = 16
PIECE = (4, 4, HID // TP, HID)
SLOTS = 4
CHUNK = 768
VMEM_LIMIT = 56 * 1024 * 1024

KEEP_ATTN = 4
KEEP_MLP = 8
GROUP = 12
CORE = 13
AT_X = 14
AT_Y = 15
AT_Z = 16
AT_YL = 17
HEAD = 18
SHIFT = 19

eps_norm = 1e-06
drop_scale = 1.0 / 0.9
far_below = -1e30
inv_root_two = 1.0 / math.sqrt(2.0)
inv_root_tau = 1.0 / math.sqrt(2.0 * math.pi)

BLK = ("x", "yl")
bf16 = jnp.bfloat16
f32 = jnp.float32


def dot(a, b, dims):
    return lax.dot_general(a, b, ((dims[0], dims[1]), ((), ())), preferred_element_type=f32)


def normalize(values):
    mean = jnp.mean(values, axis=-1, keepdims=True)
    centred = values - mean
    inverse = lax.rsqrt(jnp.mean(centred * centred, axis=-1, keepdims=True) + eps_norm)
    return (centred * inverse, inverse)


def norm_back(grad_out, normed, inverse, gain):
    scaled = grad_out * gain
    inner = (
        scaled
        - jnp.mean(scaled, axis=-1, keepdims=True)
        - normed * jnp.mean(scaled * normed, axis=-1, keepdims=True)
    )
    return (
        inverse * inner,
        jnp.sum(grad_out * normed, axis=0, keepdims=True),
        jnp.sum(grad_out, axis=0, keepdims=True),
    )


def spread(block, axes, count):
    tiled = jnp.broadcast_to(block[None], (count,) + block.shape)
    return lax.all_to_all(tiled, axes, 0, 0)


def exchange(block, axis, by_core):
    sizes = [2 if name in ("c", "yh", "yl") else 4 for name in axis]
    route = []
    for place in range(math.prod(sizes)):
        left, spots = place, {}
        if by_core is None:
            route.append((place, place ^ 1))
            continue
        for name, size in reversed(list(zip(axis, sizes))):
            left, spots[name] = divmod(left, size)
        mask = by_core[spots["c"]]
        if "yh" in spots:
            spots["yh"] ^= mask // 2
            spots["yl"] ^= mask % 2
        else:
            spots[axis[0] if axis[0] != "c" else axis[1]] ^= mask
        partner = 0
        for name, size in zip(axis, sizes):
            partner = partner * size + spots[name]
        route.append((place, partner))
    return lax.ppermute(block, axis, route)


def swap_core(block):
    return lax.ppermute(block, "c", [(0, 1), (1, 0)])


def hop_of(entry, core):
    return (entry % 2) * (1 + 2 * core) ^ (entry // 2) * (3 - 2 * core)


def doubled(block, axis, by_core):
    return jnp.concatenate([block, exchange(block, axis, by_core)])


def gather_four(block, axis):
    return doubled(doubled(block[None], axis, (1, 3)), axis, (3, 1))


def together(blocks, axes):
    blocks = [b[None] for b in blocks]
    for by_core in ((1, 3), (3, 1)):
        got = [exchange(b, axis, by_core) for b, axis in zip(blocks, axes)]
        got = lax.optimization_barrier(tuple(got))
        blocks = [jnp.concatenate([b, g]) for b, g in zip(blocks, got)]
    return blocks


def image_ids(info, places):
    return sum((info[i] <= places).astype(jnp.int32) for i in range(IMGS))


def image_scale(info, base, ids):
    flags = [info[base + i].astype(f32) * drop_scale for i in range(IMGS)]
    return sum(jnp.where(ids == i, flags[i], 0.0) for i in range(IMGS))


def places_of(start, count, axis):
    shape = (count, 1) if axis == 0 else (1, count)
    return start + lax.broadcasted_iota(jnp.int32, shape, axis)


def whole(array):
    return (array, pl.BlockSpec(array.shape, lambda *_: (0,) * array.ndim))


def made(shape, dtype):
    spec = pl.BlockSpec(shape, lambda *_: (0,) * len(shape))
    return (jax.ShapeDtypeStruct(shape, dtype), spec)


def outside(array):
    return (array, pl.BlockSpec(memory_space=pl.ANY))


def left_outside(shape, dtype):
    return (jax.ShapeDtypeStruct(shape, dtype), pl.BlockSpec(memory_space=pl.ANY))


class Stream:
    def __init__(self, pairs, sems, depth):
        self.copies = [
            pltpu.make_async_copy(source, target, sems.at[i])
            for i, (source, target) in enumerate(pairs)
        ]
        self.begun = 0
        self.done = 0
        self.depth = depth
        self.fill()

    def fill(self):
        while self.begun < min(len(self.copies), self.done + self.depth):
            self.copies[self.begun].start()
            self.begun += 1

    def take(self, count=1):
        for _ in range(count):
            self.copies[self.done].wait()
            self.done += 1
            self.fill()


def gelu_parts(u):
    cumulative = 0.5 * (1.0 + lax.erf(u * inv_root_two))
    density = jnp.exp(-0.5 * u * u) * inv_root_tau
    return (u * cumulative, cumulative + u * density)


def launch(body, grid, scalars, ins, outs, scratch, flops, moved):
    arrays = [a for a, _ in ins]
    return pl.pallas_call(
        body,
        grid_spec=pltpu.PrefetchScalarGridSpec(
            num_scalar_prefetch=1,
            grid=grid,
            in_specs=[spec for _, spec in ins],
            out_specs=[spec for _, spec in outs],
            scratch_shapes=scratch,
        ),
        out_shape=[shape for shape, _ in outs],
        compiler_params=pltpu.CompilerParams(vmem_limit_bytes=VMEM_LIMIT),
        cost_estimate=pl.CostEstimate(flops=flops, bytes_accessed=moved, transcendentals=0),
    )(scalars, *arrays)


def attend_kernel(
    info, x, w_out, gain, bias, bq, bv, out, h_out, xhat_out, x_all, h_all, xhat_all, w, block, sems
):
    row, width = x.shape
    tokens = out.shape[0]
    here = pl.multiple_of(info[GROUP] * tokens, tokens)

    parts = row // tokens
    pairs = width // (2 * PAIR)

    parts = row // tokens
    pairs = width // (2 * PAIR)
    spots = [pl.ds(i * tokens, tokens) for i in range(parts)]
    cuts = [pl.ds(t * width + i * 2 * PAIR, 2 * PAIR) for i in range(pairs) for t in range(3)]
    stream = Stream(
        [(x.at[spot], x_all.at[spot]) for spot in spots]
        + [(w_out.at[:, cut], w.at[:, cut]) for cut in cuts],
        sems,
        parts,
    )
    saves = []
    mine = image_ids(info, places_of(here, tokens, 0))
    theirs = image_ids(info, places_of(0, row, 1))
    block[...] = jnp.where(mine == theirs, 0.0, far_below)
    for i, spot in enumerate(spots):
        stream.take()
        ids = image_ids(info, places_of(i * tokens, tokens, 0))
        normed, _inverse = normalize(x_all[spot].astype(f32) * (ids < IMGS).astype(f32))
        xhat_all[spot] = normed.astype(bf16)
        h_all[spot] = (normed * gain[...] + bias[...]).astype(bf16)
        for held, target in ((h_all, h_out), (xhat_all, xhat_out)):
            save = pltpu.make_async_copy(
                held.at[spot], target.at[spot], sems.at[parts + len(cuts) + len(saves)]
            )
            saves.append(save)
    h = h_all[...]
    h_own = h_all[pl.ds(here, tokens)]
    low = lax.broadcasted_iota(jnp.int32, (tokens, PAIR), 1) < HEAD_DIM
    for i in range(width // (2 * PAIR)):
        start = i * 2 * PAIR
        end = start + 2 * PAIR
        stream.take(3)
        if i == pairs - 1:
            for save in saves:
                save.start()
        keys = dot(h, w[:, width + start : width + end], ((1,), (0,))).astype(bf16)
        values = dot(h, w[:, 2 * width + start : 2 * width + end], ((1,), (0,)))
        values = (values + bv[start:end]).astype(bf16)
        query = dot(h_own, w[:, start:end], ((1,), (0,))) + bq[start:end]
        for p in range(2):
            cut = slice(p * PAIR, (p + 1) * PAIR)
            q = query[:, cut]
            both = jnp.concatenate([jnp.where(low, q, 0.0), jnp.where(low, 0.0, q)])
            scores = dot(both.astype(bf16), keys[:, cut], ((1,), (1,))) * HEAD_DIM**-0.5
            scores = scores.reshape(2, tokens, row) + block[...][None]
            scores = scores.reshape(2 * tokens, row)
            expo = jnp.exp(scores - jnp.max(scores, axis=-1, keepdims=True))
            probs = (expo * (1.0 / jnp.sum(expo, axis=-1, keepdims=True))).astype(bf16)
            result = dot(probs, values[:, cut], ((1,), (0,)))
            out[:, start + p * PAIR : start + (p + 1) * PAIR] = jnp.where(
                low, result[:tokens], result[tokens:]
            ).astype(bf16)
    for save in saves:
        save.wait()


def attend(info, x_all, gain, bias, w_qkv, b_query, b_value, tokens):
    row, width = x_all.shape
    return launch(
        attend_kernel,
        (1,),
        info,
        [outside(x_all), outside(w_qkv), whole(gain), whole(bias), whole(b_query), whole(b_value)],
        [
            made((tokens, width), bf16),
            left_outside((row, width), bf16),
            left_outside((row, width), bf16),
        ],
        [
            pltpu.VMEM((row, width), bf16),
            pltpu.VMEM((row, width), bf16),
            pltpu.VMEM((row, width), bf16),
            pltpu.VMEM(w_qkv.shape, bf16),
            pltpu.VMEM((tokens, row), f32),
            pltpu.SemaphoreType.DMA((3 * (row // tokens) + 3 * (width // (2 * PAIR)),)),
        ],
        6 * 10**9,
        10**7,
    )


def first_head(j):
    return 3 * (j // 2) + j % 2


def mlp_kernel(
    info,
    att,
    x,
    grad_z,
    w_proj_out,
    b_proj,
    gain,
    bias,
    w_one_out,
    b_one,
    w_two_out,
    b_two,
    out,
    grad_mid,
    outgoing,
    sums,
    mid,
    normed,
    total,
    grad_h,
    w_proj,
    w_one,
    w_two,
    sems,
):
    pairs = [(w_proj_out, w_proj)]
    for c in range(FF // CHUNK):
        cut = pl.ds(c * CHUNK, CHUNK)
        pairs += [(w_one_out.at[:, cut], w_one.at[:, cut]), (w_two_out.at[cut], w_two.at[cut])]
    stream = Stream(pairs, sems, 3)
    tokens = x.shape[0]
    ids = image_ids(info, places_of(info[GROUP] * tokens, tokens, 0))
    scale_attn = image_scale(info, KEEP_ATTN, ids)
    scale_mlp = image_scale(info, KEEP_MLP, ids)
    stream.take()
    branch = dot(att[...], w_proj[...], ((1,), (0,))) + b_proj[...]
    y = x[...].astype(f32) * (ids < IMGS).astype(f32) + scale_attn * branch
    mid[...] = y
    hat, inverse = normalize(y)
    normed[...] = hat
    h_two = (hat * gain[...] + bias[...]).astype(bf16)
    grad_mlp = (scale_mlp * grad_z[...].astype(f32)).astype(bf16)
    for c in range(FF // CHUNK):
        cut = slice(c * CHUNK, (c + 1) * CHUNK)
        stream.take(2)
        hidden = dot(h_two, w_one[:, cut], ((1,), (0,))) + b_one[cut]
        grad_gelled = dot(grad_mlp, w_two[cut], ((1,), (1,)))
        gelled, slope = gelu_parts(hidden)
        grad_hidden = (grad_gelled * slope).astype(bf16)
        forth = dot(gelled.astype(bf16), w_two[cut], ((1,), (0,)))
        back = dot(grad_hidden, w_one[:, cut], ((1,), (1,)))
        if c == 0:
            total[...] = forth
            grad_h[...] = back
        else:
            total[...] += forth
            grad_h[...] += back
    out[...] = (mid[...] + scale_mlp * (total[...] + b_two[...])).astype(bf16)
    back, gain_sum, bias_sum = norm_back(grad_h[...], normed[...], inverse, gain[...])
    grad_y = grad_z[...].astype(f32) + back
    grad_mid[...] = grad_y
    sums[...] = jnp.zeros_like(sums)
    sums[0:1] = gain_sum
    sums[1:2] = bias_sum
    sums[2:3] = jnp.sum(grad_mlp.astype(f32), axis=0, keepdims=True)
    branch_t = jnp.transpose(scale_attn * grad_y).astype(bf16)
    att_t = dot(w_proj[...], branch_t, ((1,), (0,))).astype(bf16)
    for j in range(TP):
        start = first_head(j) * HEAD_DIM
        outgoing[j, :PAIR] = att_t[start : start + PAIR]
        outgoing[j, PAIR:] = branch_t[j * COLS : (j + 1) * COLS]


def mlp(info, att, x, grad_z, w_proj, b_proj, gain, bias, w_one, b_one, w_two, b_two):
    tokens, width = x.shape
    wide = (tokens, width)
    return launch(
        mlp_kernel,
        (1,),
        info,
        [
            whole(att),
            whole(x),
            whole(grad_z),
            outside(w_proj),
            whole(b_proj),
            whole(gain),
            whole(bias),
            outside(w_one),
            whole(b_one),
            outside(w_two),
            whole(b_two),
        ],
        [
            made(wide, bf16),
            made(wide, f32),
            made((TP, PAIR + COLS, tokens), bf16),
            made((8, width), f32),
        ],
        [
            pltpu.VMEM(wide, f32),
            pltpu.VMEM(wide, f32),
            pltpu.VMEM(wide, f32),
            pltpu.VMEM(wide, f32),
            pltpu.VMEM(w_proj.shape, bf16),
            pltpu.VMEM(w_one.shape, bf16),
            pltpu.VMEM(w_two.shape, bf16),
            pltpu.SemaphoreType.DMA((1 + 2 * FF // CHUNK,)),
        ],
        3 * 10**9,
        11 * 10**6,
    )


def shifted(left, right, odd):
    both = jnp.concatenate([left[:, HEAD_DIM:], right[:, :HEAD_DIM]], axis=1)
    return jnp.where(odd, both, left)


def pair_kernel(
    info,
    h_out,
    w_qkv,
    bq,
    bv,
    query,
    key_t,
    value,
    probs_out,
    w_t,
    h,
    windows,
    probs,
    keys,
    w,
    b,
    sems,
    sems_out,
):
    row, width = h.shape
    block = 256
    blocks = [pl.ds(i * block, block) for i in range(row // block)]
    odd = info[HEAD] % 2 == 1
    first = info[HEAD] // 2 * PAIR
    pairs = []
    for t in range(3):
        start = pl.multiple_of(first + t * width, PAIR)
        after = pl.multiple_of(jnp.minimum(start + PAIR, 3 * width - PAIR), PAIR)
        pairs.append((w_qkv.at[:, pl.ds(start, PAIR)], windows.at[2 * t]))
        pairs.append((w_qkv.at[:, pl.ds(after, PAIR)], windows.at[2 * t + 1]))
    pairs += [(h_out.at[spot], h.at[spot]) for spot in blocks]
    stream = Stream(pairs, sems, 6)
    for t in range(3):
        stream.take(2)
        chosen = shifted(windows[2 * t].astype(f32), windows[2 * t + 1].astype(f32), odd)
        w[:, t * PAIR : (t + 1) * PAIR] = chosen.astype(bf16)
        w_t[t * PAIR : (t + 1) * PAIR] = jnp.transpose(chosen).astype(bf16)
    for t, bias in ((0, bq), (2, bv)):
        left = bias[pl.ds(pl.multiple_of(first, PAIR), PAIR)].reshape(1, PAIR)
        after = jnp.minimum(first + PAIR, width - PAIR)
        right = bias[pl.ds(pl.multiple_of(after, PAIR), PAIR)].reshape(1, PAIR)
        b[t : t + 1] = shifted(left, right, odd)
    for i in range(row // block):
        spot = slice(i * block, (i + 1) * block)
        stream.take()
        qkv = dot(h[spot], w[...], ((1,), (0,)))
        query[spot] = (qkv[:, :PAIR] + b[0:1]).astype(bf16)
        keys[spot] = qkv[:, PAIR : 2 * PAIR].astype(bf16)
        value[spot] = (qkv[:, 2 * PAIR :] + b[2:3]).astype(bf16)
        key_t[:, spot] = jnp.transpose(qkv[:, PAIR : 2 * PAIR]).astype(bf16)
    their = image_ids(info, places_of(0, row, 0))
    k = keys[...]
    low = lax.broadcasted_iota(jnp.int32, k.shape, 1) < HEAD_DIM
    k_pair = [jnp.where(low == (e == 0), k, jnp.zeros_like(k)) for e in range(2)]
    for i in range(row // block):
        spot = slice(i * block, (i + 1) * block)
        allowed = their == image_ids(info, places_of(i * block, block, 1))
        for e in range(2):
            scores = dot(k_pair[e], query[spot], ((1,), (1,))) * HEAD_DIM**-0.5
            scores = jnp.where(allowed, scores, far_below)
            expo = jnp.exp(scores - jnp.max(scores, axis=0, keepdims=True))
            probs[i, e] = (expo * (1.0 / jnp.sum(expo, axis=0, keepdims=True))).astype(bf16)
        pltpu.make_async_copy(probs.at[i], probs_out.at[i], sems_out.at[i]).start()
    for i in range(row // block):
        pltpu.make_async_copy(probs.at[i], probs_out.at[i], sems_out.at[i]).wait()


def pair_forward(info, h_all, w_qkv, b_query, b_value):
    row, width = h_all.shape
    return launch(
        pair_kernel,
        (1,),
        info,
        [outside(h_all), outside(w_qkv), whole(b_query), whole(b_value)],
        [
            made((row, PAIR), bf16),
            made((PAIR, row), bf16),
            made((row, PAIR), bf16),
            left_outside((4, 2, row, row // 4), bf16),
            made((3 * PAIR, width), bf16),
        ],
        [
            pltpu.VMEM((row, width), bf16),
            pltpu.VMEM((6, width, PAIR), bf16),
            pltpu.VMEM((4, 2, row, row // 4), bf16),
            pltpu.VMEM((row, PAIR), bf16),
            pltpu.VMEM((width, 3 * PAIR), bf16),
            pltpu.VMEM((8, PAIR), f32),
            pltpu.SemaphoreType.DMA((10,)),
            pltpu.SemaphoreType.DMA((4,)),
        ],
        3 * 10**9,
        8 * 10**6,
    )


def pair_back_kernel(
    info,
    incoming,
    query,
    key_t,
    value,
    probs_out,
    w_t_out,
    h_out,
    xhat_out,
    grad_b,
    outgoing,
    sums,
    grad_t,
    grad_rows,
    d_t,
    d_key,
    d_value,
    flat,
    probs,
    w_t,
    h,
    xhat,
    sems,
):
    stream = Stream(
        [(probs_out.at[i], probs.at[i]) for i in range(4)]
        + [(h_out, h), (xhat_out, xhat), (w_t_out, w_t)],
        sems,
        2,
    )
    tokens = incoming.shape[2]
    row, width = h.shape
    block = 256
    for t in range(TP):
        spot = slice(t * tokens, (t + 1) * tokens)
        piece = incoming[t, :PAIR]
        grad_t[:, spot] = piece
        grad_rows[spot] = jnp.transpose(piece.astype(f32)).astype(bf16)
    v = value[...]
    low = lax.broadcasted_iota(jnp.int32, v.shape, 1) < HEAD_DIM
    v_pair = [jnp.where(low == (e == 0), v, jnp.zeros_like(v)) for e in range(2)]
    for i in range(row // block):
        spot = slice(i * block, (i + 1) * block)
        dk, dv = [], []
        stream.take()
        for e in range(2):
            p = probs[i, e]
            dp = dot(v_pair[e], grad_t[:, spot], ((1,), (0,)))
            p_wide = p.astype(f32)
            delta = jnp.sum(p_wide * dp, axis=0, keepdims=True)
            ds = (p_wide * (dp - delta)).astype(bf16)
            dk.append(dot(ds, query[spot], ((1,), (0,))))
            dv.append(dot(p, grad_rows[spot], ((1,), (0,))))
            rows = slice(e * HEAD_DIM, (e + 1) * HEAD_DIM)
            d_t[0, rows, spot] = dot(key_t[rows], ds, ((1,), (0,)))
        if i == 0:
            d_key[...] = jnp.where(low, dk[0], dk[1])
            d_value[...] = jnp.where(low, dv[0], dv[1])
        else:
            d_key[...] += jnp.where(low, dk[0], dk[1])
            d_value[...] += jnp.where(low, dv[0], dv[1])
    stream.take(3)
    scale = HEAD_DIM**-0.5
    d_t[0] = d_t[0] * scale
    d_t[1] = jnp.transpose(d_key[...]) * scale
    d_t[2] = jnp.transpose(d_value[...])
    shift = info[SHIFT]
    spot = pl.ds(pl.multiple_of(shift, HEAD_DIM // 2), COLS)
    ones = jnp.ones((8, row), bf16)
    sums[...] = jnp.zeros_like(sums)
    gain_sum = jnp.zeros((1, width), f32)
    bias_sum = jnp.zeros((1, width), f32)
    for t in range(3):
        rows = slice(t * COLS, (t + 1) * COLS)
        part = d_t[t, spot].astype(bf16)
        flat[rows] = part
        s = jnp.sum(part.astype(f32), axis=1, keepdims=True)
        sums[2 + t : 3 + t, :COLS] = dot(ones, part, ((1,), (1,)))[0:1]
        grad_b[rows] = dot(part, h[...], ((1,), (0,)))
        w = w_t[pl.ds(pl.multiple_of(t * PAIR + shift, HEAD_DIM // 2), COLS)].astype(f32)
        inner = dot(part, xhat[...], ((1,), (0,)))
        gain_sum += jnp.sum(w * inner, axis=0, keepdims=True)
        bias_sum += jnp.sum(w * s, axis=0, keepdims=True)
    for t in range(TP):
        outgoing[t] = flat[:, t * tokens : (t + 1) * tokens]
    sums[0:1] = gain_sum
    sums[1:2] = bias_sum


def pair_back(info, incoming, query, key_t, value, probs, w_t, h_all, xhat_all):
    row, width = h_all.shape
    tokens = incoming.shape[2]
    return launch(
        pair_back_kernel,
        (1,),
        info,
        [whole(incoming), whole(query), whole(key_t), whole(value)]
        + [outside(a) for a in (probs, w_t, h_all, xhat_all)],
        [
            made((3 * COLS, width), f32),
            made((TP, 3 * COLS, tokens), bf16),
            made((8, width), f32),
        ],
        [
            pltpu.VMEM((PAIR, row), bf16),
            pltpu.VMEM((row, PAIR), bf16),
            pltpu.VMEM((3, PAIR, row), f32),
            pltpu.VMEM((row, PAIR), f32),
            pltpu.VMEM((row, PAIR), f32),
            pltpu.VMEM((3 * COLS, row), bf16),
            pltpu.VMEM(probs.shape, bf16),
            pltpu.VMEM(w_t.shape, bf16),
            pltpu.VMEM((row, width), bf16),
            pltpu.VMEM((row, width), bf16),
            pltpu.SemaphoreType.DMA((7,)),
        ],
        6 * 10**9,
        10**7,
    )


def hidden_kernel(
    info,
    att_out,
    x_out,
    grad_z_out,
    incoming,
    w_proj_out,
    b_proj,
    gain,
    bias,
    w_one_out,
    b_one,
    w_two_out,
    grad_qkv_out,
    sums_one,
    sums_two,
    mine_out,
    other_out,
    att,
    x,
    grad_z,
    w_proj,
    w_one,
    w_two,
    grad_qkv,
    grad_one,
    grad_two,
    grad_proj,
    vec,
    mine,
    other,
    sems,
    sems_out,
):
    tokens = att.shape[2]
    units = pl.ds(pl.multiple_of(info[GROUP] * HID, HID), HID)
    spots = []
    for step in range(4):
        at_x = info[AT_X] ^ hop_of(step, info[CORE])
        spots.append(pl.multiple_of(at_x * 2 * tokens, 2 * tokens))
    pairs = [(w_proj_out, w_proj)]
    for step in range(4):
        rows = pl.ds(spots[step], 2 * tokens)
        pairs.append((att_out.at[step], att.at[step]))
        pairs.append((x_out.at[rows], x.at[step]))
        pairs.append((grad_z_out.at[rows], grad_z.at[step]))
        if step == 0:
            pairs += [(w_one_out.at[:, units], w_one), (w_two_out.at[units], w_two)]
    pairs.append((grad_qkv_out, grad_qkv))
    stream = Stream(pairs, sems, 5)
    vec[...] = jnp.zeros_like(vec)
    stream.take()
    for step in range(4):
        stream.take(3)
        ids = image_ids(info, places_of(spots[step], 2 * tokens, 0))
        attended = jnp.concatenate([att[step, info[AT_YL]], att[step, 1 - info[AT_YL]]])
        branch = dot(attended, w_proj[...], ((1,), (0,))) + b_proj[...]
        y = x[step].astype(f32) * (ids < IMGS).astype(f32)
        y = y + image_scale(info, KEEP_ATTN, ids) * branch
        h = (normalize(y)[0] * gain[...] + bias[...]).astype(bf16)
        if step == 0:
            stream.take(2)
        hidden = dot(h, w_one[...], ((1,), (0,))) + b_one[units]
        gelled, slope = gelu_parts(hidden)
        grad_mlp = (image_scale(info, KEEP_MLP, ids) * grad_z[step].astype(f32)).astype(bf16)
        grad_hidden = (dot(grad_mlp, w_two[...], ((1,), (1,))) * slope).astype(bf16)
        for_one = dot(h, grad_hidden, ((0,), (0,)))
        for_two = dot(gelled.astype(bf16), grad_mlp, ((0,), (0,)))
        vec[10:11] += jnp.sum(grad_hidden.astype(f32), axis=0, keepdims=True)
        ones = jnp.ones((8, tokens), bf16)
        pieces = [incoming[spots[step] // tokens + t, PAIR:] for t in range(2)]
        for piece in pieces:
            vec[13:14, :COLS] += dot(ones, piece, ((1,), (1,)))[0:1]
        for_proj = dot(jnp.concatenate(pieces, axis=1), attended, ((1,), (0,)))
        if step == 0:
            grad_one[...] = for_one
            grad_two[...] = for_two
            grad_proj[...] = for_proj
        else:
            grad_one[...] += for_one
            grad_two[...] += for_two
            grad_proj[...] += for_proj
    for i, (source, at) in enumerate(
        ((sums_one, 0), (sums_one, 1), (sums_two, 0), (sums_two, 1), (sums_two, 2))
    ):
        vec[2 * i : 2 * i + 1] = source[at : at + 1, :HID]
        vec[2 * i + 1 : 2 * i + 2] = source[at : at + 1, HID:]
    vec[11:12, :COLS] = sums_one[2:3, :COLS]
    vec[12:13, :COLS] = sums_one[4:5, :COLS]
    stream.take()
    high = HID // TP
    saves = []
    for k, (target, kept, core) in enumerate(
        ((other, other_out, 1 - info[CORE]), (mine, mine_out, info[CORE]))
    ):
        half = pl.ds(pl.multiple_of(core * HID, HID), HID)
        for p in range(TP):
            upper, t = divmod(p, 4)
            rows = pl.ds(pl.multiple_of(core * HID + p * high, high), high)
            start = upper * high
            if t < 3:
                last = grad_qkv[t * COLS + start : t * COLS + start + high, half]
            else:
                last = grad_proj[start : start + high, half]
            target[p, :high] = grad_one[rows].astype(target.dtype)
            target[p, high : 2 * high] = grad_two[p * high : (p + 1) * high, half].astype(
                target.dtype
            )
            target[p, 2 * high : 3 * high] = last.astype(target.dtype)
            target[p, 3 * high :] = vec[...].astype(target.dtype)
            save = pltpu.make_async_copy(target.at[p], kept.at[p], sems_out.at[k * TP + p])
            save.start()
            saves.append(save)
    for save in saves:
        save.wait()


def hidden_grads(
    info, att, x, grad_z, incoming, w_proj, b_proj, gain, bias, w_one, b_one, w_two, grad_qkv, sums_one, sums_two
):
    row, width = x.shape
    out = (TP, 3 * HID // TP + VEC_ROWS, HID)
    return launch(
        hidden_kernel,
        (1,),
        info,
        [
            outside(att),
            outside(x),
            outside(grad_z),
            whole(incoming),
            outside(w_proj),
            whole(b_proj),
            whole(gain),
            whole(bias),
            outside(w_one),
            whole(b_one),
            outside(w_two),
            outside(grad_qkv),
            whole(sums_one),
            whole(sums_two),
        ],
        [left_outside(out, f32), left_outside(out, bf16)],
        [
            pltpu.VMEM(att.shape, bf16),
            pltpu.VMEM((4, row // 4, width), bf16),
            pltpu.VMEM((4, row // 4, width), bf16),
            pltpu.VMEM(w_proj.shape, bf16),
            pltpu.VMEM((width, HID), bf16),
            pltpu.VMEM((HID, width), bf16),
            pltpu.VMEM(grad_qkv.shape, f32),
            pltpu.VMEM((width, HID), f32),
            pltpu.VMEM((HID, width), f32),
            pltpu.VMEM((COLS, width), f32),
            pltpu.VMEM((VEC_ROWS, HID), f32),
            pltpu.VMEM(out, f32),
            pltpu.VMEM(out, bf16),
            pltpu.SemaphoreType.DMA((16,)),
            pltpu.SemaphoreType.DMA((2 * TP,)),
        ],
        4 * 10**9,
        10**7,
    )


def input_kernel(info, incoming, w_qkv, x, grad_mid, gain, out, flat):
    tokens, width = x.shape
    for j in range(TP):
        for t in range(3):
            flat[t * width + j * COLS : t * width + (j + 1) * COLS] = incoming[
                j, t * COLS : (t + 1) * COLS
            ]
    grad_h = jnp.transpose(dot(w_qkv[...], flat[...], ((1,), (0,))))
    ids = image_ids(info, places_of(info[GROUP] * tokens, tokens, 0))
    valid = (ids < IMGS).astype(f32)
    normed, inverse = normalize(x[...].astype(f32) * valid)
    back, _gain_sum, _bias_sum = norm_back(grad_h, normed, inverse, gain[...])
    out[...] = ((grad_mid[...] + back) * valid).astype(bf16)


def input_grad(info, incoming, w_qkv, x, grad_mid, gain):
    tokens, width = x.shape
    return launch(
        input_kernel,
        (1,),
        info,
        [whole(incoming), whole(w_qkv), whole(x), whole(grad_mid), whole(gain)],
        [made((tokens, width), bf16)],
        [pltpu.VMEM((3 * width, tokens), bf16)],
        10**9,
        5 * 10**6,
    )[0]


def place_kernel(tasks, n_arrays, n_old, info, *refs):
    arrays = refs[:n_arrays]
    one, two, qkv, proj, raw, wide, split, tall, sem_in, sem_out = refs[n_arrays + n_old :]
    at = [info[AT_X], info[AT_Y], info[AT_Z]]

    def load(i):
        slot = i % SLOTS
        return pltpu.make_async_copy(arrays[tasks[i][1]], raw.at[slot], sem_in.at[slot])

    def core_of(i):
        return 1 - info[CORE] if tasks[i][3] else info[CORE]

    def store(i, begin):
        part, _, hop, _ = tasks[i]
        slot = i % SLOTS
        core = core_of(i)
        spot = at[part] ^ hop_of(hop, core)
        rows = pl.ds(pl.multiple_of(core * HID, HID), HID)
        done = sem_out.at[slot]

        def go(source, target):
            copy = pltpu.make_async_copy(source, target, done)
            if begin:
                copy.start()
            else:
                copy.wait()

        columns = pl.ds(pl.multiple_of(spot * D, D), D)
        if part == 0:
            go(wide.at[slot], one.at[rows, columns])
        elif part == 1:
            go(split.at[slot], two.at[:, spot % 2, spot // 2, :, rows])
        else:

            @pl.when(spot < 3)
            def _():
                go(wide.at[slot], qkv.at[rows, columns])

            @pl.when(spot == 3)
            def _():
                go(wide.at[slot], proj.at[rows, :])

    for i in range(min(SLOTS, len(tasks))):
        load(i).start()
    for i in range(len(tasks)):
        part = tasks[i][0]
        slot = i % SLOTS
        load(i).wait()
        if i >= SLOTS:
            store(i - SLOTS, False)
        high = PIECE[2]
        core = core_of(i)
        for outer in range(PIECE[0]):
            for inner in range(PIECE[1]):
                piece = raw[slot, outer, inner].astype(f32)
                if part == 0:
                    y, z = at[1] ^ hop_of(outer, core), at[2] ^ hop_of(inner, core)
                    start = pl.multiple_of((y // 2 * 4 + z) * high, high)
                    column = pl.multiple_of(y % 2 * HID, HID)
                    wide[slot, pl.ds(start, high), pl.ds(column, HID)] = piece
                elif part == 1:
                    x, z = at[0] ^ hop_of(outer, core), at[2] ^ hop_of(inner, core)
                    split[slot, x, pl.ds(pl.multiple_of(z * high, high), high)] = piece
                else:
                    y, x = at[1] ^ hop_of(outer, core), at[0] ^ hop_of(inner, core)
                    start = pl.multiple_of((x * 2 + y % 2) * COLS + y // 2 * high, high)
                    tall[pl.ds(start, high)] = piece
        if part == 2:
            wide[slot] = jnp.transpose(tall[...])
        store(i, True)
        if i + SLOTS < len(tasks):
            load(i + SLOTS).start()
    for i in range(max(0, len(tasks) - SLOTS), len(tasks)):
        store(i, False)


def place_pieces(info, pieces, old):
    tasks, arrays = [], []
    for part, mine, other, hop in pieces:
        for swapped, array in ((False, mine), (True, other)):
            tasks.append((part, len(arrays), hop, swapped))
            arrays.append(array)
    sds = jax.ShapeDtypeStruct
    shapes = [
        sds((D, FF), f32),
        sds((4, 2, 2, HID // 2, D), f32),
        sds((D, 3 * D), f32),
        sds((D, D), f32),
    ]
    anywhere = pl.BlockSpec(memory_space=pl.ANY)
    n_old = len(old)

    def body(*refs):
        place_kernel(tasks, len(arrays), n_old, *refs)

    return pl.pallas_call(
        body,
        grid_spec=pltpu.PrefetchScalarGridSpec(
            num_scalar_prefetch=1,
            grid=(1,),
            in_specs=[anywhere] * (len(arrays) + n_old),
            out_specs=[anywhere] * 4,
            scratch_shapes=[
                pltpu.VMEM((SLOTS,) + PIECE, bf16),
                pltpu.VMEM((SLOTS, HID, D), f32),
                pltpu.VMEM((SLOTS, 4, HID // 2, HID), f32),
                pltpu.VMEM((D, HID), f32),
                pltpu.SemaphoreType.DMA((SLOTS,)),
                pltpu.SemaphoreType.DMA((SLOTS,)),
            ],
        ),
        out_shape=shapes,
        input_output_aliases={1 + len(arrays) + i: i for i in range(n_old)},
        compiler_params=pltpu.CompilerParams(vmem_limit_bytes=VMEM_LIMIT),
        cost_estimate=pl.CostEstimate(
            flops=0, bytes_accessed=1800000 * len(tasks), transcendentals=0
        ),
    )(info, *arrays, *old)


def vector_kernel(info, gathered, *refs):
    outs, flat = refs[:9], refs[9]
    for outer in range(2):
        for inner in range(4):
            y = info[AT_Y] ^ hop_of(outer, info[CORE])
            x = info[AT_X] ^ hop_of(inner, info[CORE])
            flat[x * 2 + y % 2] = gathered[outer, inner].astype(f32)
    shared = jnp.sum(flat[...], axis=0)
    for i in range(5):
        outs[i][:HID] = shared[2 * i]
        outs[i][HID:] = shared[2 * i + 1]
    for j in range(TP):
        outs[5][j * HID : (j + 1) * HID] = flat[j, 10]
    total = jnp.zeros((VEC_ROWS, D), f32)
    source = lax.broadcasted_iota(jnp.int32, (PAIR, D), 0)
    target = lax.broadcasted_iota(jnp.int32, (PAIR, D), 1)
    for j in range(TP):
        moves = (source + j * COLS == target) & (source < COLS)
        total += dot(flat[j, :, :PAIR].astype(bf16), moves.astype(bf16), ((1,), (0,)))
    for i in range(3):
        outs[6 + i][...] = total[11 + i]


def place_vectors(info, gathered):
    block = (4, 4, VEC_ROWS, HID)
    last = gathered.shape[2] // VEC_ROWS - 1
    return launch(
        vector_kernel,
        (1,),
        info,
        [(gathered, pl.BlockSpec(block, lambda i, _: (0, 0, last, 0)))],
        [made((D,), f32)] * 5 + [made((FF,), f32)] + [made((D,), f32)] * 3,
        [pltpu.VMEM((TP, VEC_ROWS, HID), f32)],
        10**7,
        10**6,
    )


def per_device(
    layer_input,
    out_grad,
    lengths,
    keep,
    ln1_gain,
    ln1_bias,
    w_qkv,
    b_query,
    b_value,
    w_proj,
    b_proj,
    ln2_gain,
    ln2_bias,
    w_fc1,
    b_fc1,
    w_fc2,
    b_fc2,
):
    _, tokens, width = layer_input.shape
    row = tokens * TP
    group = lax.axis_index(BLK)
    places = [
        group,
        lax.axis_index("c"),
        lax.axis_index("x"),
        lax.axis_index(("yh", "yl")),
        lax.axis_index("z"),
        lax.axis_index("yl"),
        first_head(group),
        group % 2 * (HEAD_DIM // 2),
    ]
    info = jnp.concatenate(
        [jnp.cumsum(lengths[0]), keep[0, 0], keep[1, 0], jnp.stack(places).astype(jnp.int32)]
    )
    axis_x, axis_y, axis_z = ("c", "x"), ("yh", "c", "yl"), ("z", "c")

    x_all = spread(layer_input[0], BLK, TP)
    grad_z_all = jnp.broadcast_to(out_grad, (TP, tokens, width))
    x_all, grad_z_all, info = lax.optimization_barrier((x_all, grad_z_all, info))
    grad_z_all = lax.all_to_all(grad_z_all, BLK, 0, 0)
    x_all = x_all.reshape(row, width)
    attended, h_all, xhat_all = attend(
        info, x_all, ln1_gain, ln1_bias, w_qkv, b_query, b_value, tokens
    )
    by_yl = exchange(attended, ("x", "yl"), None)
    output, grad_mid, outgoing, sums_two = mlp(
        info,
        attended,
        layer_input[0],
        out_grad[0],
        w_proj,
        b_proj,
        ln2_gain,
        ln2_bias,
        w_fc1,
        b_fc1,
        w_fc2,
        b_fc2,
    )
    by_yl, outgoing, grad_z_all = lax.optimization_barrier((by_yl, outgoing, grad_z_all))
    incoming = lax.all_to_all(outgoing, BLK, 0, 0)
    attended_all = jnp.stack([attended, by_yl])[None]
    beside = exchange(attended_all, axis_x, (1, 3))
    pair = pair_forward(info, h_all, w_qkv, b_query, b_value)
    beside, pair = lax.optimization_barrier((beside, tuple(pair)))
    attended_all = doubled(jnp.concatenate([attended_all, beside]), axis_x, (3, 1))
    grad_qkv, back_out, sums_one = pair_back(info, incoming, *pair, h_all, xhat_all)
    mine, other = hidden_grads(
        info,
        attended_all,
        x_all,
        grad_z_all.reshape(row, width),
        incoming,
        w_proj,
        b_proj,
        ln2_gain,
        ln2_bias,
        w_fc1,
        b_fc1,
        w_fc2,
        grad_qkv,
        sums_one,
        sums_two,
    )
    back_in = lax.all_to_all(back_out, BLK, 0, 0)
    mine, other, back_in = lax.optimization_barrier((mine, other, back_in))

    half = (mine + swap_core(other).astype(f32)).astype(bf16)
    pieces = lax.all_to_all(half, ("yh", "z"), 0, 0)
    x_grad = input_grad(info, back_in, w_qkv, layer_input[0], grad_mid, ln1_gain)
    pieces, x_grad = lax.optimization_barrier((pieces, x_grad))
    piece = jnp.sum(pieces.astype(f32), axis=0).astype(bf16)
    high = HID // TP
    one_two, part_b = together([piece[: 2 * high], piece[2 * high :]], [axis_z, axis_x])
    part_one, part_two, part_b = together(
        [one_two[:, :high], one_two[:, high:], part_b], [axis_y, axis_x, axis_y]
    )
    parts = (part_one, part_two, part_b[:, :, :high])
    axes = (axis_x, axis_y, axis_z)

    def place(stage, old):
        return place_pieces(
            info, [(i, p, q, hop) for held, swapped, hop in stage for i, (p, q) in enumerate(zip(held, swapped))], old
        )

    near = [exchange(p, axis, (1, 3)) for p, axis in zip(parts, axes)]
    far = [exchange(p, axis, (3, 1)) for p, axis in zip(parts, axes)]
    outs = place([(parts, [swap_core(p) for p in parts], 0)], ())
    vectors = place_vectors(info, part_b)
    near, far, outs, vectors = lax.optimization_barrier((near, far, tuple(outs), tuple(vectors)))
    last = [exchange(p, axis, (3, 1)) for p, axis in zip(near, axes)]
    outs = place(
        [(near, [swap_core(p) for p in near], 1), (far, [swap_core(p) for p in far], 2)], tuple(outs)
    )
    last, outs = lax.optimization_barrier((last, tuple(outs)))
    outs = place([(last, [swap_core(p) for p in last], 3)], tuple(outs))
    grad_w_fc1, grad_w_fc2, grad_w_qkv, grad_w_proj = outs

    ln1g, ln1b, ln2g, ln2b, b_two_grad, b_one_grad, bq_grad, bv_grad, b_proj_grad = vectors
    return (
        output[None],
        x_grad[None],
        ln1g,
        ln1b,
        grad_w_qkv,
        bq_grad,
        bv_grad,
        grad_w_proj,
        b_proj_grad,
        ln2g,
        ln2b,
        grad_w_fc1,
        b_one_grad,
        grad_w_fc2.reshape(FF, D),
        b_two_grad,
    )


def solution(mesh):
    fine = Mesh(mesh.devices.reshape(2, 4, 2, 4, 2), ("yh", "z", "c", "x", "yl"))
    dp = ("yh", "z", "c")
    tokens = P(dp, BLK, None)
    placed = (tokens, tokens, P(dp, None), P(None, dp, None)) + (P(),) * 13
    return jax.shard_map(
        per_device,
        mesh=fine,
        in_specs=placed,
        out_specs=(tokens, tokens) + (P(),) * 13,
        check_vma=False,
    )
```

```python
import math

import jax
import jax.numpy as jnp
from jax import lax
from jax.experimental import pallas as pl
from jax.experimental.pallas import tpu as pltpu
from jax.sharding import Mesh
from jax.sharding import PartitionSpec as P

D = 768
HEADS = 12
HEAD_DIM = 64
FF = 3072
IMGS = 4
TP = 8
COLS = D // TP
HID = FF // TP
PAIR = 2 * HEAD_DIM
VEC_ROWS = 16
PIECE = (4, 4, HID // TP, HID)
SLOTS = 4
PLACE_LIMIT = 20 * 1024 * 1024
CHUNK = 768
VMEM_LIMIT = 56 * 1024 * 1024

KEEP_ATTN = 4
KEEP_MLP = 8
GROUP = 12
CORE = 13
AT_X = 14
AT_Y = 15
AT_Z = 16
AT_YL = 17
HEAD = 18
SHIFT = 19

eps_norm = 1e-06
drop_scale = 1.0 / 0.9
far_below = -1e30
inv_root_two = 1.0 / math.sqrt(2.0)
inv_root_tau = 1.0 / math.sqrt(2.0 * math.pi)

BLK = ("x", "yl")
bf16 = jnp.bfloat16
f32 = jnp.float32


def dot(a, b, dims):
    return lax.dot_general(a, b, ((dims[0], dims[1]), ((), ())), preferred_element_type=f32)


def normalize(values):
    mean = jnp.mean(values, axis=-1, keepdims=True)
    centred = values - mean
    inverse = lax.rsqrt(jnp.mean(centred * centred, axis=-1, keepdims=True) + eps_norm)
    return (centred * inverse, inverse)


def norm_back(grad_out, normed, inverse, gain):
    scaled = grad_out * gain
    inner = (
        scaled
        - jnp.mean(scaled, axis=-1, keepdims=True)
        - normed * jnp.mean(scaled * normed, axis=-1, keepdims=True)
    )
    return (
        inverse * inner,
        jnp.sum(grad_out * normed, axis=0, keepdims=True),
        jnp.sum(grad_out, axis=0, keepdims=True),
    )


def spread(block, axes, count):
    tiled = jnp.broadcast_to(block[None], (count,) + block.shape)
    return lax.all_to_all(tiled, axes, 0, 0)


def exchange(block, axis, by_core):
    sizes = [2 if name in ("c", "yh", "yl") else 4 for name in axis]
    route = []
    for place in range(math.prod(sizes)):
        left, spots = place, {}
        if by_core is None:
            route.append((place, place ^ 1))
            continue
        for name, size in reversed(list(zip(axis, sizes))):
            left, spots[name] = divmod(left, size)
        mask = by_core[spots["c"]]
        if "yh" in spots:
            spots["yh"] ^= mask // 2
            spots["yl"] ^= mask % 2
        else:
            spots[axis[0] if axis[0] != "c" else axis[1]] ^= mask
        partner = 0
        for name, size in zip(axis, sizes):
            partner = partner * size + spots[name]
        route.append((place, partner))
    return lax.ppermute(block, axis, route)


def swap_core(block):
    return lax.ppermute(block, "c", [(0, 1), (1, 0)])


def hop_of(entry, core):
    return (entry % 2) * (1 + 2 * core) ^ (entry // 2) * (3 - 2 * core)


def doubled(block, axis, by_core):
    return jnp.concatenate([block, exchange(block, axis, by_core)])


def gather_four(block, axis):
    return doubled(doubled(block[None], axis, (1, 3)), axis, (3, 1))


def together(blocks, axes):
    blocks = [b[None] for b in blocks]
    for by_core in ((1, 3), (3, 1)):
        got = [exchange(b, axis, by_core) for b, axis in zip(blocks, axes)]
        got = lax.optimization_barrier(tuple(got))
        blocks = [jnp.concatenate([b, g]) for b, g in zip(blocks, got)]
    return blocks


def image_ids(info, places):
    return sum((info[i] <= places).astype(jnp.int32) for i in range(IMGS))


def image_scale(info, base, ids):
    flags = [info[base + i].astype(f32) * drop_scale for i in range(IMGS)]
    return sum(jnp.where(ids == i, flags[i], 0.0) for i in range(IMGS))


def places_of(start, count, axis):
    shape = (count, 1) if axis == 0 else (1, count)
    return start + lax.broadcasted_iota(jnp.int32, shape, axis)


def whole(array):
    return (array, pl.BlockSpec(array.shape, lambda *_: (0,) * array.ndim))


def made(shape, dtype):
    spec = pl.BlockSpec(shape, lambda *_: (0,) * len(shape))
    return (jax.ShapeDtypeStruct(shape, dtype), spec)


def outside(array):
    return (array, pl.BlockSpec(memory_space=pl.ANY))


def left_outside(shape, dtype):
    return (jax.ShapeDtypeStruct(shape, dtype), pl.BlockSpec(memory_space=pl.ANY))


class Stream:
    def __init__(self, pairs, sems, depth):
        self.copies = [
            pltpu.make_async_copy(source, target, sems.at[i])
            for i, (source, target) in enumerate(pairs)
        ]
        self.begun = 0
        self.done = 0
        self.depth = depth
        self.fill()

    def fill(self):
        while self.begun < min(len(self.copies), self.done + self.depth):
            self.copies[self.begun].start()
            self.begun += 1

    def take(self, count=1):
        for _ in range(count):
            self.copies[self.done].wait()
            self.done += 1
            self.fill()


def gelu_parts(u):
    cumulative = 0.5 * (1.0 + lax.erf(u * inv_root_two))
    density = jnp.exp(-0.5 * u * u) * inv_root_tau
    return (u * cumulative, cumulative + u * density)


def launch(body, grid, scalars, ins, outs, scratch, flops, moved):
    arrays = [a for a, _ in ins]
    return pl.pallas_call(
        body,
        grid_spec=pltpu.PrefetchScalarGridSpec(
            num_scalar_prefetch=1,
            grid=grid,
            in_specs=[spec for _, spec in ins],
            out_specs=[spec for _, spec in outs],
            scratch_shapes=scratch,
        ),
        out_shape=[shape for shape, _ in outs],
        compiler_params=pltpu.CompilerParams(vmem_limit_bytes=VMEM_LIMIT),
        cost_estimate=pl.CostEstimate(flops=flops, bytes_accessed=moved, transcendentals=0),
    )(scalars, *arrays)


def attend_kernel(
    info, x, w_out, gain, bias, bq, bv, out, h_out, xhat_out, x_all, h_all, xhat_all, w, block, sems
):
    row, width = x.shape
    tokens = out.shape[0]
    here = pl.multiple_of(info[GROUP] * tokens, tokens)

    parts = row // tokens
    pairs = width // (2 * PAIR)

    parts = row // tokens
    pairs = width // (2 * PAIR)
    spots = [pl.ds(i * tokens, tokens) for i in range(parts)]
    cuts = [pl.ds(t * width + i * 2 * PAIR, 2 * PAIR) for i in range(pairs) for t in range(3)]
    stream = Stream(
        [(x.at[spot], x_all.at[spot]) for spot in spots]
        + [(w_out.at[:, cut], w.at[:, cut]) for cut in cuts],
        sems,
        parts,
    )
    saves = []
    mine = image_ids(info, places_of(here, tokens, 0))
    theirs = image_ids(info, places_of(0, row, 1))
    block[...] = jnp.where(mine == theirs, 0.0, far_below)
    for i, spot in enumerate(spots):
        stream.take()
        ids = image_ids(info, places_of(i * tokens, tokens, 0))
        normed, _inverse = normalize(x_all[spot].astype(f32) * (ids < IMGS).astype(f32))
        xhat_all[spot] = normed.astype(bf16)
        h_all[spot] = (normed * gain[...] + bias[...]).astype(bf16)
        for held, target in ((h_all, h_out), (xhat_all, xhat_out)):
            save = pltpu.make_async_copy(
                held.at[spot], target.at[spot], sems.at[parts + len(cuts) + len(saves)]
            )
            saves.append(save)
    h = h_all[...]
    h_own = h_all[pl.ds(here, tokens)]
    low = lax.broadcasted_iota(jnp.int32, (tokens, PAIR), 1) < HEAD_DIM
    for i in range(width // (2 * PAIR)):
        start = i * 2 * PAIR
        end = start + 2 * PAIR
        stream.take(3)
        if i == pairs - 1:
            for save in saves:
                save.start()
        keys = dot(h, w[:, width + start : width + end], ((1,), (0,))).astype(bf16)
        values = dot(h, w[:, 2 * width + start : 2 * width + end], ((1,), (0,)))
        values = (values + bv[start:end]).astype(bf16)
        query = dot(h_own, w[:, start:end], ((1,), (0,))) + bq[start:end]
        for p in range(2):
            cut = slice(p * PAIR, (p + 1) * PAIR)
            q = query[:, cut]
            both = jnp.concatenate([jnp.where(low, q, 0.0), jnp.where(low, 0.0, q)])
            scores = dot(both.astype(bf16), keys[:, cut], ((1,), (1,))) * HEAD_DIM**-0.5
            scores = scores.reshape(2, tokens, row) + block[...][None]
            scores = scores.reshape(2 * tokens, row)
            expo = jnp.exp(scores - jnp.max(scores, axis=-1, keepdims=True))
            probs = (expo * (1.0 / jnp.sum(expo, axis=-1, keepdims=True))).astype(bf16)
            result = dot(probs, values[:, cut], ((1,), (0,)))
            out[:, start + p * PAIR : start + (p + 1) * PAIR] = jnp.where(
                low, result[:tokens], result[tokens:]
            ).astype(bf16)
    for save in saves:
        save.wait()


def attend(info, x_all, gain, bias, w_qkv, b_query, b_value, tokens):
    row, width = x_all.shape
    return launch(
        attend_kernel,
        (1,),
        info,
        [outside(x_all), outside(w_qkv), whole(gain), whole(bias), whole(b_query), whole(b_value)],
        [
            made((tokens, width), bf16),
            left_outside((row, width), bf16),
            left_outside((row, width), bf16),
        ],
        [
            pltpu.VMEM((row, width), bf16),
            pltpu.VMEM((row, width), bf16),
            pltpu.VMEM((row, width), bf16),
            pltpu.VMEM(w_qkv.shape, bf16),
            pltpu.VMEM((tokens, row), f32),
            pltpu.SemaphoreType.DMA((3 * (row // tokens) + 3 * (width // (2 * PAIR)),)),
        ],
        6 * 10**9,
        10**7,
    )


def first_head(j):
    return 3 * (j // 2) + j % 2


def mlp_kernel(
    info,
    att,
    x,
    grad_z,
    w_proj_out,
    b_proj,
    gain,
    bias,
    w_one_out,
    b_one,
    w_two_out,
    b_two,
    out,
    grad_mid,
    outgoing,
    sums,
    mid,
    normed,
    total,
    grad_h,
    w_proj,
    w_one,
    w_two,
    sems,
):
    pairs = [(w_proj_out, w_proj)]
    for c in range(FF // CHUNK):
        cut = pl.ds(c * CHUNK, CHUNK)
        pairs += [(w_one_out.at[:, cut], w_one.at[:, cut]), (w_two_out.at[cut], w_two.at[cut])]
    stream = Stream(pairs, sems, 3)
    tokens = x.shape[0]
    ids = image_ids(info, places_of(info[GROUP] * tokens, tokens, 0))
    scale_attn = image_scale(info, KEEP_ATTN, ids)
    scale_mlp = image_scale(info, KEEP_MLP, ids)
    stream.take()
    branch = dot(att[...], w_proj[...], ((1,), (0,))) + b_proj[...]
    y = x[...].astype(f32) * (ids < IMGS).astype(f32) + scale_attn * branch
    mid[...] = y
    hat, inverse = normalize(y)
    normed[...] = hat
    h_two = (hat * gain[...] + bias[...]).astype(bf16)
    grad_mlp = (scale_mlp * grad_z[...].astype(f32)).astype(bf16)
    for c in range(FF // CHUNK):
        cut = slice(c * CHUNK, (c + 1) * CHUNK)
        stream.take(2)
        hidden = dot(h_two, w_one[:, cut], ((1,), (0,))) + b_one[cut]
        grad_gelled = dot(grad_mlp, w_two[cut], ((1,), (1,)))
        gelled, slope = gelu_parts(hidden)
        grad_hidden = (grad_gelled * slope).astype(bf16)
        forth = dot(gelled.astype(bf16), w_two[cut], ((1,), (0,)))
        back = dot(grad_hidden, w_one[:, cut], ((1,), (1,)))
        if c == 0:
            total[...] = forth
            grad_h[...] = back
        else:
            total[...] += forth
            grad_h[...] += back
    out[...] = (mid[...] + scale_mlp * (total[...] + b_two[...])).astype(bf16)
    back, gain_sum, bias_sum = norm_back(grad_h[...], normed[...], inverse, gain[...])
    grad_y = grad_z[...].astype(f32) + back
    grad_mid[...] = grad_y
    sums[...] = jnp.zeros_like(sums)
    sums[0:1] = gain_sum
    sums[1:2] = bias_sum
    sums[2:3] = jnp.sum(grad_mlp.astype(f32), axis=0, keepdims=True)
    branch_t = jnp.transpose(scale_attn * grad_y).astype(bf16)
    att_t = dot(w_proj[...], branch_t, ((1,), (0,))).astype(bf16)
    for j in range(TP):
        start = first_head(j) * HEAD_DIM
        outgoing[j, :PAIR] = att_t[start : start + PAIR]
        outgoing[j, PAIR:] = branch_t[j * COLS : (j + 1) * COLS]


def mlp(info, att, x, grad_z, w_proj, b_proj, gain, bias, w_one, b_one, w_two, b_two):
    tokens, width = x.shape
    wide = (tokens, width)
    return launch(
        mlp_kernel,
        (1,),
        info,
        [
            whole(att),
            whole(x),
            whole(grad_z),
            outside(w_proj),
            whole(b_proj),
            whole(gain),
            whole(bias),
            outside(w_one),
            whole(b_one),
            outside(w_two),
            whole(b_two),
        ],
        [
            made(wide, bf16),
            made(wide, f32),
            made((TP, PAIR + COLS, tokens), bf16),
            made((8, width), f32),
        ],
        [
            pltpu.VMEM(wide, f32),
            pltpu.VMEM(wide, f32),
            pltpu.VMEM(wide, f32),
            pltpu.VMEM(wide, f32),
            pltpu.VMEM(w_proj.shape, bf16),
            pltpu.VMEM(w_one.shape, bf16),
            pltpu.VMEM(w_two.shape, bf16),
            pltpu.SemaphoreType.DMA((1 + 2 * FF // CHUNK,)),
        ],
        3 * 10**9,
        11 * 10**6,
    )


def shifted(left, right, odd):
    both = jnp.concatenate([left[:, HEAD_DIM:], right[:, :HEAD_DIM]], axis=1)
    return jnp.where(odd, both, left)


def pair_kernel(
    info,
    h_out,
    w_qkv,
    bq,
    bv,
    query,
    key_t,
    value,
    probs_out,
    w_t,
    h,
    windows,
    probs,
    keys,
    w,
    b,
    sems,
    sems_out,
):
    row, width = h.shape
    block = 256
    blocks = [pl.ds(i * block, block) for i in range(row // block)]
    odd = info[HEAD] % 2 == 1
    first = info[HEAD] // 2 * PAIR
    pairs = []
    for t in range(3):
        start = pl.multiple_of(first + t * width, PAIR)
        after = pl.multiple_of(jnp.minimum(start + PAIR, 3 * width - PAIR), PAIR)
        pairs.append((w_qkv.at[:, pl.ds(start, PAIR)], windows.at[2 * t]))
        pairs.append((w_qkv.at[:, pl.ds(after, PAIR)], windows.at[2 * t + 1]))
    pairs += [(h_out.at[spot], h.at[spot]) for spot in blocks]
    stream = Stream(pairs, sems, 6)
    for t in range(3):
        stream.take(2)
        chosen = shifted(windows[2 * t].astype(f32), windows[2 * t + 1].astype(f32), odd)
        w[:, t * PAIR : (t + 1) * PAIR] = chosen.astype(bf16)
        w_t[t * PAIR : (t + 1) * PAIR] = jnp.transpose(chosen).astype(bf16)
    for t, bias in ((0, bq), (2, bv)):
        left = bias[pl.ds(pl.multiple_of(first, PAIR), PAIR)].reshape(1, PAIR)
        after = jnp.minimum(first + PAIR, width - PAIR)
        right = bias[pl.ds(pl.multiple_of(after, PAIR), PAIR)].reshape(1, PAIR)
        b[t : t + 1] = shifted(left, right, odd)
    for i in range(row // block):
        spot = slice(i * block, (i + 1) * block)
        stream.take()
        qkv = dot(h[spot], w[...], ((1,), (0,)))
        query[spot] = (qkv[:, :PAIR] + b[0:1]).astype(bf16)
        keys[spot] = qkv[:, PAIR : 2 * PAIR].astype(bf16)
        value[spot] = (qkv[:, 2 * PAIR :] + b[2:3]).astype(bf16)
        key_t[:, spot] = jnp.transpose(qkv[:, PAIR : 2 * PAIR]).astype(bf16)
    their = image_ids(info, places_of(0, row, 0))
    k = keys[...]
    low = lax.broadcasted_iota(jnp.int32, k.shape, 1) < HEAD_DIM
    k_pair = [jnp.where(low == (e == 0), k, jnp.zeros_like(k)) for e in range(2)]
    for i in range(row // block):
        spot = slice(i * block, (i + 1) * block)
        allowed = their == image_ids(info, places_of(i * block, block, 1))
        for e in range(2):
            scores = dot(k_pair[e], query[spot], ((1,), (1,))) * HEAD_DIM**-0.5
            scores = jnp.where(allowed, scores, far_below)
            expo = jnp.exp(scores - jnp.max(scores, axis=0, keepdims=True))
            probs[i, e] = (expo * (1.0 / jnp.sum(expo, axis=0, keepdims=True))).astype(bf16)
        pltpu.make_async_copy(probs.at[i], probs_out.at[i], sems_out.at[i]).start()
    for i in range(row // block):
        pltpu.make_async_copy(probs.at[i], probs_out.at[i], sems_out.at[i]).wait()


def pair_forward(info, h_all, w_qkv, b_query, b_value):
    row, width = h_all.shape
    return launch(
        pair_kernel,
        (1,),
        info,
        [outside(h_all), outside(w_qkv), whole(b_query), whole(b_value)],
        [
            made((row, PAIR), bf16),
            made((PAIR, row), bf16),
            made((row, PAIR), bf16),
            left_outside((4, 2, row, row // 4), bf16),
            made((3 * PAIR, width), bf16),
        ],
        [
            pltpu.VMEM((row, width), bf16),
            pltpu.VMEM((6, width, PAIR), bf16),
            pltpu.VMEM((4, 2, row, row // 4), bf16),
            pltpu.VMEM((row, PAIR), bf16),
            pltpu.VMEM((width, 3 * PAIR), bf16),
            pltpu.VMEM((8, PAIR), f32),
            pltpu.SemaphoreType.DMA((10,)),
            pltpu.SemaphoreType.DMA((4,)),
        ],
        3 * 10**9,
        8 * 10**6,
    )


def pair_back_kernel(
    info,
    incoming,
    query,
    key_t,
    value,
    probs_out,
    w_t_out,
    h_out,
    xhat_out,
    grad_b,
    outgoing,
    sums,
    grad_t,
    grad_rows,
    d_t,
    d_key,
    d_value,
    flat,
    probs,
    w_t,
    h,
    xhat,
    sems,
):
    stream = Stream(
        [(probs_out.at[i], probs.at[i]) for i in range(4)]
        + [(h_out, h), (xhat_out, xhat), (w_t_out, w_t)],
        sems,
        2,
    )
    tokens = incoming.shape[2]
    row, width = h.shape
    block = 256
    for t in range(TP):
        spot = slice(t * tokens, (t + 1) * tokens)
        piece = incoming[t, :PAIR]
        grad_t[:, spot] = piece
        grad_rows[spot] = jnp.transpose(piece.astype(f32)).astype(bf16)
    v = value[...]
    low = lax.broadcasted_iota(jnp.int32, v.shape, 1) < HEAD_DIM
    v_pair = [jnp.where(low == (e == 0), v, jnp.zeros_like(v)) for e in range(2)]
    for i in range(row // block):
        spot = slice(i * block, (i + 1) * block)
        dk, dv = [], []
        stream.take()
        for e in range(2):
            p = probs[i, e]
            dp = dot(v_pair[e], grad_t[:, spot], ((1,), (0,)))
            p_wide = p.astype(f32)
            delta = jnp.sum(p_wide * dp, axis=0, keepdims=True)
            ds = (p_wide * (dp - delta)).astype(bf16)
            dk.append(dot(ds, query[spot], ((1,), (0,))))
            dv.append(dot(p, grad_rows[spot], ((1,), (0,))))
            rows = slice(e * HEAD_DIM, (e + 1) * HEAD_DIM)
            d_t[0, rows, spot] = dot(key_t[rows], ds, ((1,), (0,)))
        if i == 0:
            d_key[...] = jnp.where(low, dk[0], dk[1])
            d_value[...] = jnp.where(low, dv[0], dv[1])
        else:
            d_key[...] += jnp.where(low, dk[0], dk[1])
            d_value[...] += jnp.where(low, dv[0], dv[1])
    stream.take(3)
    scale = HEAD_DIM**-0.5
    d_t[0] = d_t[0] * scale
    d_t[1] = jnp.transpose(d_key[...]) * scale
    d_t[2] = jnp.transpose(d_value[...])
    shift = info[SHIFT]
    spot = pl.ds(pl.multiple_of(shift, HEAD_DIM // 2), COLS)
    ones = jnp.ones((8, row), bf16)
    sums[...] = jnp.zeros_like(sums)
    for t in range(3):
        rows = slice(t * COLS, (t + 1) * COLS)
        flat[rows] = d_t[t, spot].astype(bf16)
        sums[2 + t : 3 + t, :COLS] = dot(ones, flat[rows], ((1,), (1,)))[0:1]
    grad_b[...] = dot(flat[...], h[...], ((1,), (0,)))
    inner = dot(flat[...], xhat[...], ((1,), (0,)))
    totals = jnp.sum(flat[...].astype(f32), axis=1, keepdims=True)
    gain_sum = jnp.zeros((1, width), f32)
    bias_sum = jnp.zeros((1, width), f32)
    for t in range(3):
        rows = slice(t * COLS, (t + 1) * COLS)
        w = w_t[pl.ds(pl.multiple_of(t * PAIR + shift, HEAD_DIM // 2), COLS)].astype(f32)
        gain_sum += jnp.sum(w * inner[rows], axis=0, keepdims=True)
        bias_sum += jnp.sum(w * totals[rows], axis=0, keepdims=True)
    for t in range(TP):
        outgoing[t] = flat[:, t * tokens : (t + 1) * tokens]
    sums[0:1] = gain_sum
    sums[1:2] = bias_sum


def pair_back(info, incoming, query, key_t, value, probs, w_t, h_all, xhat_all):
    row, width = h_all.shape
    tokens = incoming.shape[2]
    return launch(
        pair_back_kernel,
        (1,),
        info,
        [whole(incoming), whole(query), whole(key_t), whole(value)]
        + [outside(a) for a in (probs, w_t, h_all, xhat_all)],
        [
            made((3 * COLS, width), f32),
            made((TP, 3 * COLS, tokens), bf16),
            made((8, width), f32),
        ],
        [
            pltpu.VMEM((PAIR, row), bf16),
            pltpu.VMEM((row, PAIR), bf16),
            pltpu.VMEM((3, PAIR, row), f32),
            pltpu.VMEM((row, PAIR), f32),
            pltpu.VMEM((row, PAIR), f32),
            pltpu.VMEM((3 * COLS, row), bf16),
            pltpu.VMEM(probs.shape, bf16),
            pltpu.VMEM(w_t.shape, bf16),
            pltpu.VMEM((row, width), bf16),
            pltpu.VMEM((row, width), bf16),
            pltpu.SemaphoreType.DMA((7,)),
        ],
        6 * 10**9,
        10**7,
    )


def hidden_kernel(
    info,
    att_out,
    x_out,
    grad_z_out,
    incoming,
    w_proj_out,
    b_proj,
    gain,
    bias,
    w_one_out,
    b_one,
    w_two_out,
    grad_qkv_out,
    sums_one,
    sums_two,
    mine_out,
    other_out,
    att,
    x,
    grad_z,
    w_proj,
    w_one,
    w_two,
    grad_qkv,
    grad_one,
    grad_two,
    grad_proj,
    vec,
    mine,
    other,
    sems,
    sems_out,
):
    tokens = att.shape[2]
    units = pl.ds(pl.multiple_of(info[GROUP] * HID, HID), HID)
    spots = []
    for step in range(4):
        at_x = info[AT_X] ^ hop_of(step, info[CORE])
        spots.append(pl.multiple_of(at_x * 2 * tokens, 2 * tokens))
    pairs = [(w_proj_out, w_proj)]
    for step in range(4):
        rows = pl.ds(spots[step], 2 * tokens)
        pairs.append((att_out.at[step], att.at[step]))
        pairs.append((x_out.at[rows], x.at[step]))
        pairs.append((grad_z_out.at[rows], grad_z.at[step]))
        if step == 0:
            pairs += [(w_one_out.at[:, units], w_one), (w_two_out.at[units], w_two)]
    pairs.append((grad_qkv_out, grad_qkv))
    stream = Stream(pairs, sems, 5)
    vec[...] = jnp.zeros_like(vec)
    stream.take()
    for step in range(4):
        stream.take(3)
        ids = image_ids(info, places_of(spots[step], 2 * tokens, 0))
        attended = jnp.concatenate([att[step, info[AT_YL]], att[step, 1 - info[AT_YL]]])
        branch = dot(attended, w_proj[...], ((1,), (0,))) + b_proj[...]
        y = x[step].astype(f32) * (ids < IMGS).astype(f32)
        y = y + image_scale(info, KEEP_ATTN, ids) * branch
        h = (normalize(y)[0] * gain[...] + bias[...]).astype(bf16)
        if step == 0:
            stream.take(2)
        hidden = dot(h, w_one[...], ((1,), (0,))) + b_one[units]
        gelled, slope = gelu_parts(hidden)
        grad_mlp = (image_scale(info, KEEP_MLP, ids) * grad_z[step].astype(f32)).astype(bf16)
        grad_hidden = (dot(grad_mlp, w_two[...], ((1,), (1,))) * slope).astype(bf16)
        for_one = dot(h, grad_hidden, ((0,), (0,)))
        for_two = dot(gelled.astype(bf16), grad_mlp, ((0,), (0,)))
        vec[10:11] += jnp.sum(grad_hidden.astype(f32), axis=0, keepdims=True)
        ones = jnp.ones((8, tokens), bf16)
        pieces = [incoming[spots[step] // tokens + t, PAIR:] for t in range(2)]
        for piece in pieces:
            vec[13:14, :COLS] += dot(ones, piece, ((1,), (1,)))[0:1]
        for_proj = dot(jnp.concatenate(pieces, axis=1), attended, ((1,), (0,)))
        if step == 0:
            grad_one[...] = for_one
            grad_two[...] = for_two
            grad_proj[...] = for_proj
        else:
            grad_one[...] += for_one
            grad_two[...] += for_two
            grad_proj[...] += for_proj
    for i, (source, at) in enumerate(
        ((sums_one, 0), (sums_one, 1), (sums_two, 0), (sums_two, 1), (sums_two, 2))
    ):
        vec[2 * i : 2 * i + 1] = source[at : at + 1, :HID]
        vec[2 * i + 1 : 2 * i + 2] = source[at : at + 1, HID:]
    vec[11:12, :COLS] = sums_one[2:3, :COLS]
    vec[12:13, :COLS] = sums_one[4:5, :COLS]
    stream.take()
    high = HID // TP
    saves = []
    for k, (target, kept, core) in enumerate(
        ((other, other_out, 1 - info[CORE]), (mine, mine_out, info[CORE]))
    ):
        half = pl.ds(pl.multiple_of(core * HID, HID), HID)
        for p in range(TP):
            upper, t = divmod(p, 4)
            rows = pl.ds(pl.multiple_of(core * HID + p * high, high), high)
            start = upper * high
            if t < 3:
                last = grad_qkv[t * COLS + start : t * COLS + start + high, half]
            else:
                last = grad_proj[start : start + high, half]
            target[p, :high] = grad_one[rows].astype(target.dtype)
            target[p, high : 2 * high] = grad_two[p * high : (p + 1) * high, half].astype(
                target.dtype
            )
            target[p, 2 * high : 3 * high] = last.astype(target.dtype)
            target[p, 3 * high :] = vec[...].astype(target.dtype)
            save = pltpu.make_async_copy(target.at[p], kept.at[p], sems_out.at[k * TP + p])
            save.start()
            saves.append(save)
    for save in saves:
        save.wait()


def hidden_grads(
    info, att, x, grad_z, incoming, w_proj, b_proj, gain, bias, w_one, b_one, w_two, grad_qkv, sums_one, sums_two
):
    row, width = x.shape
    out = (TP, 3 * HID // TP + VEC_ROWS, HID)
    return launch(
        hidden_kernel,
        (1,),
        info,
        [
            outside(att),
            outside(x),
            outside(grad_z),
            whole(incoming),
            outside(w_proj),
            whole(b_proj),
            whole(gain),
            whole(bias),
            outside(w_one),
            whole(b_one),
            outside(w_two),
            outside(grad_qkv),
            whole(sums_one),
            whole(sums_two),
        ],
        [left_outside(out, bf16), left_outside(out, bf16)],
        [
            pltpu.VMEM(att.shape, bf16),
            pltpu.VMEM((4, row // 4, width), bf16),
            pltpu.VMEM((4, row // 4, width), bf16),
            pltpu.VMEM(w_proj.shape, bf16),
            pltpu.VMEM((width, HID), bf16),
            pltpu.VMEM((HID, width), bf16),
            pltpu.VMEM(grad_qkv.shape, f32),
            pltpu.VMEM((width, HID), f32),
            pltpu.VMEM((HID, width), f32),
            pltpu.VMEM((COLS, width), f32),
            pltpu.VMEM((VEC_ROWS, HID), f32),
            pltpu.VMEM(out, bf16),
            pltpu.VMEM(out, bf16),
            pltpu.SemaphoreType.DMA((16,)),
            pltpu.SemaphoreType.DMA((2 * TP,)),
        ],
        4 * 10**9,
        10**7,
    )


def input_kernel(info, incoming, w_qkv, x, grad_mid, gain, out, flat):
    tokens, width = x.shape
    for j in range(TP):
        for t in range(3):
            flat[t * width + j * COLS : t * width + (j + 1) * COLS] = incoming[
                j, t * COLS : (t + 1) * COLS
            ]
    grad_h = jnp.transpose(dot(w_qkv[...], flat[...], ((1,), (0,))))
    ids = image_ids(info, places_of(info[GROUP] * tokens, tokens, 0))
    valid = (ids < IMGS).astype(f32)
    normed, inverse = normalize(x[...].astype(f32) * valid)
    back, _gain_sum, _bias_sum = norm_back(grad_h, normed, inverse, gain[...])
    out[...] = ((grad_mid[...] + back) * valid).astype(bf16)


def input_grad(info, incoming, w_qkv, x, grad_mid, gain):
    tokens, width = x.shape
    return launch(
        input_kernel,
        (1,),
        info,
        [whole(incoming), whole(w_qkv), whole(x), whole(grad_mid), whole(gain)],
        [made((tokens, width), bf16)],
        [pltpu.VMEM((3 * width, tokens), bf16)],
        10**9,
        5 * 10**6,
    )[0]


def place_kernel(tasks, n_arrays, n_old, info, *refs):
    arrays = refs[:n_arrays]
    one, two, qkv, proj, raw, wide, split, tall, sem_in, sem_out = refs[n_arrays + n_old :]
    at = [info[AT_X], info[AT_Y], info[AT_Z]]

    def load(i):
        slot = i % SLOTS
        return pltpu.make_async_copy(arrays[tasks[i][1]], raw.at[slot], sem_in.at[slot])

    def core_of(i):
        return 1 - info[CORE] if tasks[i][3] else info[CORE]

    def store(i, begin):
        part, _, hop, _ = tasks[i]
        slot = i % SLOTS
        core = core_of(i)
        spot = at[part] ^ hop_of(hop, core)
        rows = pl.ds(pl.multiple_of(core * HID, HID), HID)
        done = sem_out.at[slot]

        def go(source, target):
            copy = pltpu.make_async_copy(source, target, done)
            if begin:
                copy.start()
            else:
                copy.wait()

        columns = pl.ds(pl.multiple_of(spot * D, D), D)
        if part == 0:
            go(wide.at[slot], one.at[rows, columns])
        elif part == 1:
            go(split.at[slot], two.at[:, spot % 2, spot // 2, :, rows])
        else:

            @pl.when(spot < 3)
            def _():
                go(wide.at[slot], qkv.at[rows, columns])

            @pl.when(spot == 3)
            def _():
                go(wide.at[slot], proj.at[rows, :])

    for i in range(min(SLOTS, len(tasks))):
        load(i).start()
    for i in range(len(tasks)):
        part = tasks[i][0]
        slot = i % SLOTS
        load(i).wait()
        if i >= SLOTS:
            store(i - SLOTS, False)
        high = PIECE[2]
        core = core_of(i)
        for outer in range(PIECE[0]):
            for inner in range(PIECE[1]):
                piece = raw[slot, outer, inner].astype(f32)
                if part == 0:
                    y, z = at[1] ^ hop_of(outer, core), at[2] ^ hop_of(inner, core)
                    start = pl.multiple_of((y // 2 * 4 + z) * high, high)
                    column = pl.multiple_of(y % 2 * HID, HID)
                    wide[slot, pl.ds(start, high), pl.ds(column, HID)] = piece
                elif part == 1:
                    x, z = at[0] ^ hop_of(outer, core), at[2] ^ hop_of(inner, core)
                    split[slot, x, pl.ds(pl.multiple_of(z * high, high), high)] = piece
                else:
                    y, x = at[1] ^ hop_of(outer, core), at[0] ^ hop_of(inner, core)
                    start = pl.multiple_of((x * 2 + y % 2) * COLS + y // 2 * high, high)
                    tall[pl.ds(start, high)] = piece
        if part == 2:
            wide[slot] = jnp.transpose(tall[...])
        store(i, True)
        if i + SLOTS < len(tasks):
            load(i + SLOTS).start()
    for i in range(max(0, len(tasks) - SLOTS), len(tasks)):
        store(i, False)


def place_pieces(info, pieces, old):
    tasks, arrays = [], []
    for part, mine, other, hop in pieces:
        for swapped, array in ((False, mine), (True, other)):
            tasks.append((part, len(arrays), hop, swapped))
            arrays.append(array)
    sds = jax.ShapeDtypeStruct
    shapes = [
        sds((D, FF), f32),
        sds((4, 2, 2, HID // 2, D), f32),
        sds((D, 3 * D), f32),
        sds((D, D), f32),
    ]
    anywhere = pl.BlockSpec(memory_space=pl.ANY)
    n_old = len(old)

    def body(*refs):
        place_kernel(tasks, len(arrays), n_old, *refs)

    return pl.pallas_call(
        body,
        grid_spec=pltpu.PrefetchScalarGridSpec(
            num_scalar_prefetch=1,
            grid=(1,),
            in_specs=[anywhere] * (len(arrays) + n_old),
            out_specs=[anywhere] * 4,
            scratch_shapes=[
                pltpu.VMEM((SLOTS,) + PIECE, bf16),
                pltpu.VMEM((SLOTS, HID, D), f32),
                pltpu.VMEM((SLOTS, 4, HID // 2, HID), f32),
                pltpu.VMEM((D, HID), f32),
                pltpu.SemaphoreType.DMA((SLOTS,)),
                pltpu.SemaphoreType.DMA((SLOTS,)),
            ],
        ),
        out_shape=shapes,
        input_output_aliases={1 + len(arrays) + i: i for i in range(n_old)},
        compiler_params=pltpu.CompilerParams(vmem_limit_bytes=PLACE_LIMIT),
        cost_estimate=pl.CostEstimate(
            flops=0, bytes_accessed=1800000 * len(tasks), transcendentals=0
        ),
    )(info, *arrays, *old)


def vector_kernel(info, gathered, *refs):
    outs, flat = refs[:9], refs[9]
    for outer in range(2):
        for inner in range(4):
            y = info[AT_Y] ^ hop_of(outer, info[CORE])
            x = info[AT_X] ^ hop_of(inner, info[CORE])
            flat[x * 2 + y % 2] = gathered[outer, inner].astype(f32)
    shared = jnp.sum(flat[...], axis=0)
    for i in range(5):
        outs[i][:HID] = shared[2 * i]
        outs[i][HID:] = shared[2 * i + 1]
    for j in range(TP):
        outs[5][j * HID : (j + 1) * HID] = flat[j, 10]
    total = jnp.zeros((VEC_ROWS, D), f32)
    source = lax.broadcasted_iota(jnp.int32, (PAIR, D), 0)
    target = lax.broadcasted_iota(jnp.int32, (PAIR, D), 1)
    for j in range(TP):
        moves = (source + j * COLS == target) & (source < COLS)
        total += dot(flat[j, :, :PAIR].astype(bf16), moves.astype(bf16), ((1,), (0,)))
    for i in range(3):
        outs[6 + i][...] = total[11 + i]


def place_vectors(info, gathered):
    block = (4, 4, VEC_ROWS, HID)
    last = gathered.shape[2] // VEC_ROWS - 1
    return launch(
        vector_kernel,
        (1,),
        info,
        [(gathered, pl.BlockSpec(block, lambda i, _: (0, 0, last, 0)))],
        [made((D,), f32)] * 5 + [made((FF,), f32)] + [made((D,), f32)] * 3,
        [pltpu.VMEM((TP, VEC_ROWS, HID), f32)],
        10**7,
        10**6,
    )


def per_device(
    layer_input,
    out_grad,
    lengths,
    keep,
    ln1_gain,
    ln1_bias,
    w_qkv,
    b_query,
    b_value,
    w_proj,
    b_proj,
    ln2_gain,
    ln2_bias,
    w_fc1,
    b_fc1,
    w_fc2,
    b_fc2,
):
    _, tokens, width = layer_input.shape
    row = tokens * TP
    group = lax.axis_index(BLK)
    places = [
        group,
        lax.axis_index("c"),
        lax.axis_index("x"),
        lax.axis_index(("yh", "yl")),
        lax.axis_index("z"),
        lax.axis_index("yl"),
        first_head(group),
        group % 2 * (HEAD_DIM // 2),
    ]
    info = jnp.concatenate(
        [jnp.cumsum(lengths[0]), keep[0, 0], keep[1, 0], jnp.stack(places).astype(jnp.int32)]
    )
    axis_x, axis_y, axis_z = ("c", "x"), ("yh", "c", "yl"), ("z", "c")

    x_all = spread(layer_input[0], BLK, TP)
    grad_z_all = jnp.broadcast_to(out_grad, (TP, tokens, width))
    x_all, grad_z_all, info = lax.optimization_barrier((x_all, grad_z_all, info))
    grad_z_all = lax.all_to_all(grad_z_all, BLK, 0, 0)
    x_all = x_all.reshape(row, width)
    attended, h_all, xhat_all = attend(
        info, x_all, ln1_gain, ln1_bias, w_qkv, b_query, b_value, tokens
    )
    by_yl = exchange(attended, ("x", "yl"), None)
    output, grad_mid, outgoing, sums_two = mlp(
        info,
        attended,
        layer_input[0],
        out_grad[0],
        w_proj,
        b_proj,
        ln2_gain,
        ln2_bias,
        w_fc1,
        b_fc1,
        w_fc2,
        b_fc2,
    )
    by_yl, outgoing, grad_z_all = lax.optimization_barrier((by_yl, outgoing, grad_z_all))
    incoming = lax.all_to_all(outgoing, BLK, 0, 0)
    attended_all = jnp.stack([attended, by_yl])[None]
    beside = exchange(attended_all, axis_x, (1, 3))
    pair = pair_forward(info, h_all, w_qkv, b_query, b_value)
    beside, pair = lax.optimization_barrier((beside, tuple(pair)))
    attended_all = doubled(jnp.concatenate([attended_all, beside]), axis_x, (3, 1))
    grad_qkv, back_out, sums_one = pair_back(info, incoming, *pair, h_all, xhat_all)
    mine, other = hidden_grads(
        info,
        attended_all,
        x_all,
        grad_z_all.reshape(row, width),
        incoming,
        w_proj,
        b_proj,
        ln2_gain,
        ln2_bias,
        w_fc1,
        b_fc1,
        w_fc2,
        grad_qkv,
        sums_one,
        sums_two,
    )
    back_in = lax.all_to_all(back_out, BLK, 0, 0)
    mine, other, back_in = lax.optimization_barrier((mine, other, back_in))

    half = (mine.astype(f32) + swap_core(other).astype(f32)).astype(bf16)
    pieces = lax.all_to_all(half, ("yh", "z"), 0, 0)
    x_grad = input_grad(info, back_in, w_qkv, layer_input[0], grad_mid, ln1_gain)
    pieces, x_grad = lax.optimization_barrier((pieces, x_grad))
    piece = jnp.sum(pieces.astype(f32), axis=0).astype(bf16)
    high = HID // TP
    one_two, part_b = together([piece[: 2 * high], piece[2 * high :]], [axis_z, axis_x])
    along_y = jnp.concatenate([one_two[:, :high], part_b], axis=1)
    along_y, part_two = together([along_y, one_two[:, high:]], [axis_y, axis_x])
    parts = (along_y[:, :, :high], part_two, along_y[:, :, high : 2 * high])
    axes = (axis_x, axis_y, axis_z)

    def place(stage, old):
        return place_pieces(
            info, [(i, p, q, hop) for held, swapped, hop in stage for i, (p, q) in enumerate(zip(held, swapped))], old
        )

    fence = lax.optimization_barrier

    def hop(pieces, by_core):
        return [exchange(p, axis, by_core) for p, axis in zip(pieces, axes)]

    def swapped(pieces):
        return [swap_core(p) for p in pieces]

    parts, beside = fence((parts, swapped(parts)))
    near, far = hop(parts, (1, 3)), hop(parts, (3, 1))
    vectors = tuple(place_vectors(info, along_y))
    near, vectors = fence((near, vectors))
    last, near_beside = hop(near, (3, 1)), swapped(near)
    outs = tuple(place([(parts, beside, 0)], ()))
    far, near_beside, outs = fence((far, near_beside, outs))
    far_beside = swapped(far)
    outs = tuple(place([(near, near_beside, 1)], outs))
    last, far_beside, outs = fence((last, far_beside, outs))
    last_beside = swapped(last)
    outs = tuple(place([(far, far_beside, 2)], outs))
    last_beside, outs = fence((last_beside, outs))
    outs = place([(last, last_beside, 3)], outs)
    grad_w_fc1, grad_w_fc2, grad_w_qkv, grad_w_proj = outs

    ln1g, ln1b, ln2g, ln2b, b_two_grad, b_one_grad, bq_grad, bv_grad, b_proj_grad = vectors
    return (
        output[None],
        x_grad[None],
        ln1g,
        ln1b,
        grad_w_qkv,
        bq_grad,
        bv_grad,
        grad_w_proj,
        b_proj_grad,
        ln2g,
        ln2b,
        grad_w_fc1,
        b_one_grad,
        grad_w_fc2.reshape(FF, D),
        b_two_grad,
    )


def solution(mesh):
    fine = Mesh(mesh.devices.reshape(2, 4, 2, 4, 2), ("yh", "z", "c", "x", "yl"))
    dp = ("yh", "z", "c")
    tokens = P(dp, BLK, None)
    placed = (tokens, tokens, P(dp, None), P(None, dp, None)) + (P(),) * 13
    return jax.shard_map(
        per_device,
        mesh=fine,
        in_specs=placed,
        out_specs=(tokens, tokens) + (P(),) * 13,
        check_vma=False,
    )
```

```python
import math

import jax
import jax.numpy as jnp
from jax import lax
from jax.experimental import pallas as pl
from jax.experimental.pallas import tpu as pltpu
from jax.sharding import Mesh
from jax.sharding import PartitionSpec as P

D = 768
HEADS = 12
HEAD_DIM = 64
FF = 3072
IMGS = 4
TP = 8
COLS = D // TP
HID = FF // TP
PAIR = 2 * HEAD_DIM
VEC_ROWS = 16
PIECE = (4, 4, HID // TP, HID)
SLOTS = 4
PLACE_LIMIT = 20 * 1024 * 1024
CHUNK = 768
VMEM_LIMIT = 56 * 1024 * 1024

KEEP_ATTN = 4
KEEP_MLP = 8
GROUP = 12
CORE = 13
AT_X = 14
AT_Y = 15
AT_Z = 16
AT_YL = 17
HEAD = 18
SHIFT = 19

eps_norm = 1e-06
drop_scale = 1.0 / 0.9
far_below = -1e30
inv_root_two = 1.0 / math.sqrt(2.0)
inv_root_tau = 1.0 / math.sqrt(2.0 * math.pi)

BLK = ("x", "yl")
bf16 = jnp.bfloat16
f32 = jnp.float32


def dot(a, b, dims):
    return lax.dot_general(a, b, ((dims[0], dims[1]), ((), ())), preferred_element_type=f32)


def normalize(values):
    mean = jnp.mean(values, axis=-1, keepdims=True)
    centred = values - mean
    inverse = lax.rsqrt(jnp.mean(centred * centred, axis=-1, keepdims=True) + eps_norm)
    return (centred * inverse, inverse)


def norm_back(grad_out, normed, inverse, gain):
    scaled = grad_out * gain
    inner = (
        scaled
        - jnp.mean(scaled, axis=-1, keepdims=True)
        - normed * jnp.mean(scaled * normed, axis=-1, keepdims=True)
    )
    return (
        inverse * inner,
        jnp.sum(grad_out * normed, axis=0, keepdims=True),
        jnp.sum(grad_out, axis=0, keepdims=True),
    )


def spread(block, axes, count):
    tiled = jnp.broadcast_to(block[None], (count,) + block.shape)
    return lax.all_to_all(tiled, axes, 0, 0)


def exchange(block, axis, by_core):
    sizes = [2 if name in ("c", "yh", "yl") else 4 for name in axis]
    route = []
    for place in range(math.prod(sizes)):
        left, spots = place, {}
        if by_core is None:
            route.append((place, place ^ 1))
            continue
        for name, size in reversed(list(zip(axis, sizes))):
            left, spots[name] = divmod(left, size)
        mask = by_core[spots["c"]]
        if "yh" in spots:
            spots["yh"] ^= mask // 2
            spots["yl"] ^= mask % 2
        else:
            spots[axis[0] if axis[0] != "c" else axis[1]] ^= mask
        partner = 0
        for name, size in zip(axis, sizes):
            partner = partner * size + spots[name]
        route.append((place, partner))
    return lax.ppermute(block, axis, route)


def swap_core(block):
    return lax.ppermute(block, "c", [(0, 1), (1, 0)])


def hop_of(entry, core):
    return (entry % 2) * (1 + 2 * core) ^ (entry // 2) * (3 - 2 * core)


def doubled(block, axis, by_core):
    return jnp.concatenate([block, exchange(block, axis, by_core)])


def gather_four(block, axis):
    return doubled(doubled(block[None], axis, (1, 3)), axis, (3, 1))


def together(blocks, axes):
    blocks = [b[None] for b in blocks]
    for by_core in ((1, 3), (3, 1)):
        got = [exchange(b, axis, by_core) for b, axis in zip(blocks, axes)]
        got = lax.optimization_barrier(tuple(got))
        blocks = [jnp.concatenate([b, g]) for b, g in zip(blocks, got)]
    return blocks


def image_ids(info, places):
    return sum((info[i] <= places).astype(jnp.int32) for i in range(IMGS))


def image_scale(info, base, ids):
    flags = [info[base + i].astype(f32) * drop_scale for i in range(IMGS)]
    return sum(jnp.where(ids == i, flags[i], 0.0) for i in range(IMGS))


def places_of(start, count, axis):
    shape = (count, 1) if axis == 0 else (1, count)
    return start + lax.broadcasted_iota(jnp.int32, shape, axis)


def whole(array):
    return (array, pl.BlockSpec(array.shape, lambda *_: (0,) * array.ndim))


def made(shape, dtype):
    spec = pl.BlockSpec(shape, lambda *_: (0,) * len(shape))
    return (jax.ShapeDtypeStruct(shape, dtype), spec)


def outside(array):
    return (array, pl.BlockSpec(memory_space=pl.ANY))


def left_outside(shape, dtype):
    return (jax.ShapeDtypeStruct(shape, dtype), pl.BlockSpec(memory_space=pl.ANY))


class Stream:
    def __init__(self, pairs, sems, depth):
        self.copies = [
            pltpu.make_async_copy(source, target, sems.at[i])
            for i, (source, target) in enumerate(pairs)
        ]
        self.begun = 0
        self.done = 0
        self.depth = depth
        self.fill()

    def fill(self):
        while self.begun < min(len(self.copies), self.done + self.depth):
            self.copies[self.begun].start()
            self.begun += 1

    def take(self, count=1):
        for _ in range(count):
            self.copies[self.done].wait()
            self.done += 1
            self.fill()


def gelu_parts(u):
    cumulative = 0.5 * (1.0 + lax.erf(u * inv_root_two))
    density = jnp.exp(-0.5 * u * u) * inv_root_tau
    return (u * cumulative, cumulative + u * density)


def launch(body, grid, scalars, ins, outs, scratch, flops, moved):
    arrays = [a for a, _ in ins]
    return pl.pallas_call(
        body,
        grid_spec=pltpu.PrefetchScalarGridSpec(
            num_scalar_prefetch=1,
            grid=grid,
            in_specs=[spec for _, spec in ins],
            out_specs=[spec for _, spec in outs],
            scratch_shapes=scratch,
        ),
        out_shape=[shape for shape, _ in outs],
        compiler_params=pltpu.CompilerParams(vmem_limit_bytes=VMEM_LIMIT),
        cost_estimate=pl.CostEstimate(flops=flops, bytes_accessed=moved, transcendentals=0),
    )(scalars, *arrays)


def attend_kernel(
    info, x, w_out, gain, bias, bq, bv, out, h_out, xhat_out, x_all, h_all, xhat_all, w, block, sems
):
    row, width = x.shape
    tokens = out.shape[0]
    here = pl.multiple_of(info[GROUP] * tokens, tokens)

    parts = row // tokens
    pairs = width // (2 * PAIR)

    parts = row // tokens
    pairs = width // (2 * PAIR)
    spots = [pl.ds(i * tokens, tokens) for i in range(parts)]
    cuts = [pl.ds(t * width + i * 2 * PAIR, 2 * PAIR) for i in range(pairs) for t in range(3)]
    stream = Stream(
        [(x.at[spot], x_all.at[spot]) for spot in spots]
        + [(w_out.at[:, cut], w.at[:, cut]) for cut in cuts],
        sems,
        parts,
    )
    saves = []
    mine = image_ids(info, places_of(here, tokens, 0))
    theirs = image_ids(info, places_of(0, row, 1))
    block[...] = jnp.where(mine == theirs, 0.0, far_below)
    for i, spot in enumerate(spots):
        stream.take()
        ids = image_ids(info, places_of(i * tokens, tokens, 0))
        normed, _inverse = normalize(x_all[spot].astype(f32) * (ids < IMGS).astype(f32))
        xhat_all[spot] = normed.astype(bf16)
        h_all[spot] = (normed * gain[...] + bias[...]).astype(bf16)
        for held, target in ((h_all, h_out), (xhat_all, xhat_out)):
            save = pltpu.make_async_copy(
                held.at[spot], target.at[spot], sems.at[parts + len(cuts) + len(saves)]
            )
            saves.append(save)
    h = h_all[...]
    h_own = h_all[pl.ds(here, tokens)]
    low = lax.broadcasted_iota(jnp.int32, (tokens, PAIR), 1) < HEAD_DIM
    for i in range(width // (2 * PAIR)):
        start = i * 2 * PAIR
        end = start + 2 * PAIR
        stream.take(3)
        if i == pairs - 1:
            for save in saves:
                save.start()
        keys = dot(h, w[:, width + start : width + end], ((1,), (0,))).astype(bf16)
        values = dot(h, w[:, 2 * width + start : 2 * width + end], ((1,), (0,)))
        values = (values + bv[start:end]).astype(bf16)
        query = (dot(h_own, w[:, start:end], ((1,), (0,))) + bq[start:end]) * HEAD_DIM**-0.5
        for p in range(2):
            cut = slice(p * PAIR, (p + 1) * PAIR)
            q = query[:, cut]
            both = jnp.concatenate([jnp.where(low, q, 0.0), jnp.where(low, 0.0, q)])
            scores = dot(both.astype(bf16), keys[:, cut], ((1,), (1,)))
            scores = scores.reshape(2, tokens, row) + block[...][None]
            scores = scores.reshape(2 * tokens, row)
            expo = jnp.exp(scores - jnp.max(scores, axis=-1, keepdims=True))
            probs = (expo * (1.0 / jnp.sum(expo, axis=-1, keepdims=True))).astype(bf16)
            result = dot(probs, values[:, cut], ((1,), (0,)))
            out[:, start + p * PAIR : start + (p + 1) * PAIR] = jnp.where(
                low, result[:tokens], result[tokens:]
            ).astype(bf16)
    for save in saves:
        save.wait()


def attend(info, x_all, gain, bias, w_qkv, b_query, b_value, tokens):
    row, width = x_all.shape
    return launch(
        attend_kernel,
        (1,),
        info,
        [outside(x_all), outside(w_qkv), whole(gain), whole(bias), whole(b_query), whole(b_value)],
        [
            made((tokens, width), bf16),
            left_outside((row, width), bf16),
            left_outside((row, width), bf16),
        ],
        [
            pltpu.VMEM((row, width), bf16),
            pltpu.VMEM((row, width), bf16),
            pltpu.VMEM((row, width), bf16),
            pltpu.VMEM(w_qkv.shape, bf16),
            pltpu.VMEM((tokens, row), f32),
            pltpu.SemaphoreType.DMA((3 * (row // tokens) + 3 * (width // (2 * PAIR)),)),
        ],
        6 * 10**9,
        10**7,
    )


def first_head(j):
    return 3 * (j // 2) + j % 2


def mlp_kernel(
    info,
    att,
    x,
    grad_z,
    w_proj_out,
    b_proj,
    gain,
    bias,
    w_one_out,
    b_one,
    w_two_out,
    b_two,
    out,
    grad_mid,
    outgoing,
    sums,
    mid,
    normed,
    total,
    grad_h,
    w_proj,
    w_one,
    w_two,
    sems,
):
    pairs = [(w_proj_out, w_proj)]
    for c in range(FF // CHUNK):
        cut = pl.ds(c * CHUNK, CHUNK)
        pairs += [(w_one_out.at[:, cut], w_one.at[:, cut]), (w_two_out.at[cut], w_two.at[cut])]
    stream = Stream(pairs, sems, len(pairs))
    tokens = x.shape[0]
    ids = image_ids(info, places_of(info[GROUP] * tokens, tokens, 0))
    scale_attn = image_scale(info, KEEP_ATTN, ids)
    scale_mlp = image_scale(info, KEEP_MLP, ids)
    stream.take()
    branch = dot(att[...], w_proj[...], ((1,), (0,))) + b_proj[...]
    y = x[...].astype(f32) * (ids < IMGS).astype(f32) + scale_attn * branch
    mid[...] = y
    hat, inverse = normalize(y)
    normed[...] = hat
    h_two = (hat * gain[...] + bias[...]).astype(bf16)
    grad_mlp = (scale_mlp * grad_z[...].astype(f32)).astype(bf16)
    for c in range(FF // CHUNK):
        cut = slice(c * CHUNK, (c + 1) * CHUNK)
        stream.take(2)
        hidden = dot(h_two, w_one[:, cut], ((1,), (0,))) + b_one[cut]
        grad_gelled = dot(grad_mlp, w_two[cut], ((1,), (1,)))
        gelled, slope = gelu_parts(hidden)
        grad_hidden = (grad_gelled * slope).astype(bf16)
        forth = dot(gelled.astype(bf16), w_two[cut], ((1,), (0,)))
        back = dot(grad_hidden, w_one[:, cut], ((1,), (1,)))
        if c == 0:
            total[...] = forth
            grad_h[...] = back
        else:
            total[...] += forth
            grad_h[...] += back
    out[...] = (mid[...] + scale_mlp * (total[...] + b_two[...])).astype(bf16)
    back, gain_sum, bias_sum = norm_back(grad_h[...], normed[...], inverse, gain[...])
    grad_y = grad_z[...].astype(f32) + back
    grad_mid[...] = grad_y
    sums[...] = jnp.zeros_like(sums)
    sums[0:1] = gain_sum
    sums[1:2] = bias_sum
    sums[2:3] = jnp.sum(grad_mlp.astype(f32), axis=0, keepdims=True)
    branch_t = jnp.transpose(scale_attn * grad_y).astype(bf16)
    att_t = dot(w_proj[...], branch_t, ((1,), (0,))).astype(bf16)
    for j in range(TP):
        start = first_head(j) * HEAD_DIM
        outgoing[j, :PAIR] = att_t[start : start + PAIR]
        outgoing[j, PAIR:] = branch_t[j * COLS : (j + 1) * COLS]


def mlp(info, att, x, grad_z, w_proj, b_proj, gain, bias, w_one, b_one, w_two, b_two):
    tokens, width = x.shape
    wide = (tokens, width)
    return launch(
        mlp_kernel,
        (1,),
        info,
        [
            whole(att),
            whole(x),
            whole(grad_z),
            outside(w_proj),
            whole(b_proj),
            whole(gain),
            whole(bias),
            outside(w_one),
            whole(b_one),
            outside(w_two),
            whole(b_two),
        ],
        [
            made(wide, bf16),
            made(wide, f32),
            made((TP, PAIR + COLS, tokens), bf16),
            made((8, width), f32),
        ],
        [
            pltpu.VMEM(wide, f32),
            pltpu.VMEM(wide, f32),
            pltpu.VMEM(wide, f32),
            pltpu.VMEM(wide, f32),
            pltpu.VMEM(w_proj.shape, bf16),
            pltpu.VMEM(w_one.shape, bf16),
            pltpu.VMEM(w_two.shape, bf16),
            pltpu.SemaphoreType.DMA((1 + 2 * FF // CHUNK,)),
        ],
        3 * 10**9,
        11 * 10**6,
    )


def shifted(left, right, odd):
    both = jnp.concatenate([left[:, HEAD_DIM:], right[:, :HEAD_DIM]], axis=1)
    return jnp.where(odd, both, left)


def pair_kernel(
    info,
    h_out,
    w_qkv,
    bq,
    bv,
    query,
    key_t,
    value,
    probs_out,
    w_t,
    h,
    windows,
    probs,
    keys,
    w,
    b,
    sems,
    sems_out,
):
    row, width = h.shape
    block = 256
    blocks = [pl.ds(i * block, block) for i in range(row // block)]
    odd = info[HEAD] % 2 == 1
    first = info[HEAD] // 2 * PAIR
    pairs = []
    for t in range(3):
        start = pl.multiple_of(first + t * width, PAIR)
        after = pl.multiple_of(jnp.minimum(start + PAIR, 3 * width - PAIR), PAIR)
        pairs.append((w_qkv.at[:, pl.ds(start, PAIR)], windows.at[2 * t]))
        pairs.append((w_qkv.at[:, pl.ds(after, PAIR)], windows.at[2 * t + 1]))
    pairs += [(h_out.at[spot], h.at[spot]) for spot in blocks]
    stream = Stream(pairs, sems, 6)
    for t in range(3):
        stream.take(2)
        chosen = shifted(windows[2 * t].astype(f32), windows[2 * t + 1].astype(f32), odd)
        w[:, t * PAIR : (t + 1) * PAIR] = chosen.astype(bf16)
        w_t[t * PAIR : (t + 1) * PAIR] = jnp.transpose(chosen).astype(bf16)
    for t, bias in ((0, bq), (2, bv)):
        left = bias[pl.ds(pl.multiple_of(first, PAIR), PAIR)].reshape(1, PAIR)
        after = jnp.minimum(first + PAIR, width - PAIR)
        right = bias[pl.ds(pl.multiple_of(after, PAIR), PAIR)].reshape(1, PAIR)
        b[t : t + 1] = shifted(left, right, odd)
    for i in range(row // block):
        spot = slice(i * block, (i + 1) * block)
        stream.take()
        qkv = dot(h[spot], w[...], ((1,), (0,)))
        query[spot] = ((qkv[:, :PAIR] + b[0:1]) * HEAD_DIM**-0.5).astype(bf16)
        keys[spot] = qkv[:, PAIR : 2 * PAIR].astype(bf16)
        value[spot] = (qkv[:, 2 * PAIR :] + b[2:3]).astype(bf16)
        key_t[:, spot] = jnp.transpose(qkv[:, PAIR : 2 * PAIR]).astype(bf16)
    their = image_ids(info, places_of(0, row, 0))
    k = keys[...]
    low = lax.broadcasted_iota(jnp.int32, k.shape, 1) < HEAD_DIM
    k_pair = [jnp.where(low == (e == 0), k, jnp.zeros_like(k)) for e in range(2)]
    for i in range(row // block):
        spot = slice(i * block, (i + 1) * block)
        allowed = their == image_ids(info, places_of(i * block, block, 1))
        for e in range(2):
            scores = dot(k_pair[e], query[spot], ((1,), (1,)))
            scores = jnp.where(allowed, scores, far_below)
            expo = jnp.exp(scores - jnp.max(scores, axis=0, keepdims=True))
            probs[i, e] = (expo * (1.0 / jnp.sum(expo, axis=0, keepdims=True))).astype(bf16)
        pltpu.make_async_copy(probs.at[i], probs_out.at[i], sems_out.at[i]).start()
    for i in range(row // block):
        pltpu.make_async_copy(probs.at[i], probs_out.at[i], sems_out.at[i]).wait()


def pair_forward(info, h_all, w_qkv, b_query, b_value):
    row, width = h_all.shape
    return launch(
        pair_kernel,
        (1,),
        info,
        [outside(h_all), outside(w_qkv), whole(b_query), whole(b_value)],
        [
            made((row, PAIR), bf16),
            made((PAIR, row), bf16),
            made((row, PAIR), bf16),
            left_outside((4, 2, row, row // 4), bf16),
            made((3 * PAIR, width), bf16),
        ],
        [
            pltpu.VMEM((row, width), bf16),
            pltpu.VMEM((6, width, PAIR), bf16),
            pltpu.VMEM((4, 2, row, row // 4), bf16),
            pltpu.VMEM((row, PAIR), bf16),
            pltpu.VMEM((width, 3 * PAIR), bf16),
            pltpu.VMEM((8, PAIR), f32),
            pltpu.SemaphoreType.DMA((10,)),
            pltpu.SemaphoreType.DMA((4,)),
        ],
        3 * 10**9,
        8 * 10**6,
    )


def pair_back_kernel(
    info,
    incoming,
    query,
    key_t,
    value,
    probs_out,
    w_t_out,
    h_out,
    xhat_out,
    grad_b,
    outgoing,
    sums,
    grad_t,
    grad_rows,
    d_t,
    d_key,
    d_value,
    flat,
    probs,
    w_t,
    h,
    xhat,
    sems,
):
    stream = Stream(
        [(probs_out.at[i], probs.at[i]) for i in range(4)]
        + [(h_out, h), (xhat_out, xhat), (w_t_out, w_t)],
        sems,
        7,
    )
    tokens = incoming.shape[2]
    row, width = h.shape
    block = 256
    for t in range(TP):
        spot = slice(t * tokens, (t + 1) * tokens)
        piece = incoming[t, :PAIR]
        grad_t[:, spot] = piece
        grad_rows[spot] = jnp.transpose(piece.astype(f32)).astype(bf16)
    v = value[...]
    low = lax.broadcasted_iota(jnp.int32, v.shape, 1) < HEAD_DIM
    v_pair = [jnp.where(low == (e == 0), v, jnp.zeros_like(v)) for e in range(2)]
    for i in range(row // block):
        spot = slice(i * block, (i + 1) * block)
        dk, dv = [], []
        stream.take()
        for e in range(2):
            p = probs[i, e]
            dp = dot(v_pair[e], grad_t[:, spot], ((1,), (0,)))
            p_wide = p.astype(f32)
            delta = jnp.sum(p_wide * dp, axis=0, keepdims=True)
            ds = (p_wide * (dp - delta)).astype(bf16)
            dk.append(dot(ds, query[spot], ((1,), (0,))))
            dv.append(dot(p, grad_rows[spot], ((1,), (0,))))
            rows = slice(e * HEAD_DIM, (e + 1) * HEAD_DIM)
            d_t[0, rows, spot] = dot(key_t[rows], ds, ((1,), (0,)))
        if i == 0:
            d_key[...] = jnp.where(low, dk[0], dk[1])
            d_value[...] = jnp.where(low, dv[0], dv[1])
        else:
            d_key[...] += jnp.where(low, dk[0], dk[1])
            d_value[...] += jnp.where(low, dv[0], dv[1])
    stream.take(3)
    d_t[0] = d_t[0] * HEAD_DIM**-0.5
    d_t[1] = jnp.transpose(d_key[...])
    d_t[2] = jnp.transpose(d_value[...])
    shift = info[SHIFT]
    spot = pl.ds(pl.multiple_of(shift, HEAD_DIM // 2), COLS)
    ones = jnp.ones((8, row), bf16)
    sums[...] = jnp.zeros_like(sums)
    for t in range(3):
        rows = slice(t * COLS, (t + 1) * COLS)
        flat[rows] = d_t[t, spot].astype(bf16)
        sums[2 + t : 3 + t, :COLS] = dot(ones, flat[rows], ((1,), (1,)))[0:1]
    grad_b[...] = dot(flat[...], h[...], ((1,), (0,)))
    inner = dot(flat[...], xhat[...], ((1,), (0,)))
    totals = jnp.sum(flat[...].astype(f32), axis=1, keepdims=True)
    gain_sum = jnp.zeros((1, width), f32)
    bias_sum = jnp.zeros((1, width), f32)
    for t in range(3):
        rows = slice(t * COLS, (t + 1) * COLS)
        w = w_t[pl.ds(pl.multiple_of(t * PAIR + shift, HEAD_DIM // 2), COLS)].astype(f32)
        gain_sum += jnp.sum(w * inner[rows], axis=0, keepdims=True)
        bias_sum += jnp.sum(w * totals[rows], axis=0, keepdims=True)
    for t in range(TP):
        outgoing[t] = flat[:, t * tokens : (t + 1) * tokens]
    sums[0:1] = gain_sum
    sums[1:2] = bias_sum


def pair_back(info, incoming, query, key_t, value, probs, w_t, h_all, xhat_all):
    row, width = h_all.shape
    tokens = incoming.shape[2]
    return launch(
        pair_back_kernel,
        (1,),
        info,
        [whole(incoming), whole(query), whole(key_t), whole(value)]
        + [outside(a) for a in (probs, w_t, h_all, xhat_all)],
        [
            made((3 * COLS, width), f32),
            made((TP, 3 * COLS, tokens), bf16),
            made((8, width), f32),
        ],
        [
            pltpu.VMEM((PAIR, row), bf16),
            pltpu.VMEM((row, PAIR), bf16),
            pltpu.VMEM((3, PAIR, row), f32),
            pltpu.VMEM((row, PAIR), f32),
            pltpu.VMEM((row, PAIR), f32),
            pltpu.VMEM((3 * COLS, row), bf16),
            pltpu.VMEM(probs.shape, bf16),
            pltpu.VMEM(w_t.shape, bf16),
            pltpu.VMEM((row, width), bf16),
            pltpu.VMEM((row, width), bf16),
            pltpu.SemaphoreType.DMA((7,)),
        ],
        6 * 10**9,
        10**7,
    )


def hidden_kernel(
    info,
    att_near,
    att_far,
    x_out,
    grad_z_out,
    incoming,
    w_proj_out,
    b_proj,
    gain,
    bias,
    w_one_out,
    b_one,
    w_two_out,
    grad_qkv_out,
    sums_one,
    sums_two,
    mine_out,
    other_out,
    att,
    x,
    grad_z,
    w_proj,
    w_one,
    w_two,
    grad_qkv,
    grad_one,
    grad_two,
    grad_proj,
    vec,
    mine,
    other,
    sems,
    sems_out,
):
    tokens = att.shape[2]
    units = pl.ds(pl.multiple_of(info[GROUP] * HID, HID), HID)
    spots = []
    for step in range(4):
        at_x = info[AT_X] ^ hop_of(step, info[CORE])
        spots.append(pl.multiple_of(at_x * 2 * tokens, 2 * tokens))
    pairs = [(w_proj_out, w_proj)]
    for step in range(4):
        rows = pl.ds(spots[step], 2 * tokens)
        held = att_near if step < 2 else att_far
        pairs.append((held.at[step % 2], att.at[step]))
        pairs.append((x_out.at[rows], x.at[step]))
        pairs.append((grad_z_out.at[rows], grad_z.at[step]))
        if step == 0:
            pairs += [(w_one_out.at[:, units], w_one), (w_two_out.at[units], w_two)]
    pairs.append((grad_qkv_out, grad_qkv))
    stream = Stream(pairs, sems, 5)
    vec[...] = jnp.zeros_like(vec)
    stream.take()
    for step in range(4):
        stream.take(3)
        ids = image_ids(info, places_of(spots[step], 2 * tokens, 0))
        attended = jnp.concatenate([att[step, info[AT_YL]], att[step, 1 - info[AT_YL]]])
        branch = dot(attended, w_proj[...], ((1,), (0,))) + b_proj[...]
        y = x[step].astype(f32) * (ids < IMGS).astype(f32)
        y = y + image_scale(info, KEEP_ATTN, ids) * branch
        h = (normalize(y)[0] * gain[...] + bias[...]).astype(bf16)
        if step == 0:
            stream.take(2)
        hidden = dot(h, w_one[...], ((1,), (0,))) + b_one[units]
        gelled, slope = gelu_parts(hidden)
        grad_mlp = (image_scale(info, KEEP_MLP, ids) * grad_z[step].astype(f32)).astype(bf16)
        grad_hidden = (dot(grad_mlp, w_two[...], ((1,), (1,))) * slope).astype(bf16)
        for_one = dot(h, grad_hidden, ((0,), (0,)))
        for_two = dot(gelled.astype(bf16), grad_mlp, ((0,), (0,)))
        vec[10:11] += jnp.sum(grad_hidden.astype(f32), axis=0, keepdims=True)
        ones = jnp.ones((8, tokens), bf16)
        pieces = [incoming[spots[step] // tokens + t, PAIR:] for t in range(2)]
        for piece in pieces:
            vec[13:14, :COLS] += dot(ones, piece, ((1,), (1,)))[0:1]
        for_proj = dot(jnp.concatenate(pieces, axis=1), attended, ((1,), (0,)))
        if step == 0:
            grad_one[...] = for_one
            grad_two[...] = for_two
            grad_proj[...] = for_proj
        else:
            grad_one[...] += for_one
            grad_two[...] += for_two
            grad_proj[...] += for_proj
    for i, (source, at) in enumerate(
        ((sums_one, 0), (sums_one, 1), (sums_two, 0), (sums_two, 1), (sums_two, 2))
    ):
        vec[2 * i : 2 * i + 1] = source[at : at + 1, :HID]
        vec[2 * i + 1 : 2 * i + 2] = source[at : at + 1, HID:]
    vec[11:12, :COLS] = sums_one[2:3, :COLS]
    vec[12:13, :COLS] = sums_one[4:5, :COLS]
    stream.take()
    high = HID // TP
    saves = []
    for k, (target, kept, core) in enumerate(
        ((other, other_out, 1 - info[CORE]), (mine, mine_out, info[CORE]))
    ):
        half = pl.ds(pl.multiple_of(core * HID, HID), HID)
        for p in range(TP):
            upper, t = divmod(p, 4)
            rows = pl.ds(pl.multiple_of(core * HID + p * high, high), high)
            start = upper * high
            if t < 3:
                last = grad_qkv[t * COLS + start : t * COLS + start + high, half]
            else:
                last = grad_proj[start : start + high, half]
            target[p, :high] = grad_one[rows].astype(target.dtype)
            target[p, high : 2 * high] = grad_two[p * high : (p + 1) * high, half].astype(
                target.dtype
            )
            target[p, 2 * high : 3 * high] = last.astype(target.dtype)
            target[p, 3 * high :] = vec[...].astype(target.dtype)
            save = pltpu.make_async_copy(target.at[p], kept.at[p], sems_out.at[k * TP + p])
            save.start()
            saves.append(save)
    for save in saves:
        save.wait()


def hidden_grads(
    info, att, att_far, x, grad_z, incoming, w_proj, b_proj, gain, bias, w_one, b_one, w_two, grad_qkv, sums_one, sums_two
):
    row, width = x.shape
    out = (TP, 3 * HID // TP + VEC_ROWS, HID)
    return launch(
        hidden_kernel,
        (1,),
        info,
        [
            outside(att),
            outside(att_far),
            outside(x),
            outside(grad_z),
            whole(incoming),
            outside(w_proj),
            whole(b_proj),
            whole(gain),
            whole(bias),
            outside(w_one),
            whole(b_one),
            outside(w_two),
            outside(grad_qkv),
            whole(sums_one),
            whole(sums_two),
        ],
        [left_outside(out, bf16), left_outside(out, bf16)],
        [
            pltpu.VMEM((4,) + att.shape[1:], bf16),
            pltpu.VMEM((4, row // 4, width), bf16),
            pltpu.VMEM((4, row // 4, width), bf16),
            pltpu.VMEM(w_proj.shape, bf16),
            pltpu.VMEM((width, HID), bf16),
            pltpu.VMEM((HID, width), bf16),
            pltpu.VMEM(grad_qkv.shape, f32),
            pltpu.VMEM((width, HID), f32),
            pltpu.VMEM((HID, width), f32),
            pltpu.VMEM((COLS, width), f32),
            pltpu.VMEM((VEC_ROWS, HID), f32),
            pltpu.VMEM(out, bf16),
            pltpu.VMEM(out, bf16),
            pltpu.SemaphoreType.DMA((16,)),
            pltpu.SemaphoreType.DMA((2 * TP,)),
        ],
        4 * 10**9,
        10**7,
    )


def input_kernel(info, incoming, w_qkv, x, grad_mid, gain, out, flat):
    tokens, width = x.shape
    for j in range(TP):
        for t in range(3):
            flat[t * width + j * COLS : t * width + (j + 1) * COLS] = incoming[
                j, t * COLS : (t + 1) * COLS
            ]
    grad_h = jnp.transpose(dot(w_qkv[...], flat[...], ((1,), (0,))))
    ids = image_ids(info, places_of(info[GROUP] * tokens, tokens, 0))
    valid = (ids < IMGS).astype(f32)
    normed, inverse = normalize(x[...].astype(f32) * valid)
    back, _gain_sum, _bias_sum = norm_back(grad_h, normed, inverse, gain[...])
    out[...] = ((grad_mid[...] + back) * valid).astype(bf16)


def input_grad(info, incoming, w_qkv, x, grad_mid, gain):
    tokens, width = x.shape
    return launch(
        input_kernel,
        (1,),
        info,
        [whole(incoming), whole(w_qkv), whole(x), whole(grad_mid), whole(gain)],
        [made((tokens, width), bf16)],
        [pltpu.VMEM((3 * width, tokens), bf16)],
        10**9,
        5 * 10**6,
    )[0]


def place_kernel(tasks, n_arrays, n_old, info, *refs):
    arrays = refs[:n_arrays]
    one, two, qkv, proj, raw, wide, split, tall, sem_in, sem_out = refs[n_arrays + n_old :]
    at = [info[AT_X], info[AT_Y], info[AT_Z]]

    def load(i):
        slot = i % SLOTS
        part, array, _, _ = tasks[i]
        source = arrays[array]
        if len(source.shape) > 4:
            source = source.at[part]
        return pltpu.make_async_copy(source, raw.at[slot], sem_in.at[slot])

    def core_of(i):
        return 1 - info[CORE] if tasks[i][3] else info[CORE]

    def store(i, begin):
        part, _, hop, _ = tasks[i]
        slot = i % SLOTS
        core = core_of(i)
        spot = at[part] ^ hop_of(hop, core)
        rows = pl.ds(pl.multiple_of(core * HID, HID), HID)
        done = sem_out.at[slot]

        def go(source, target):
            copy = pltpu.make_async_copy(source, target, done)
            if begin:
                copy.start()
            else:
                copy.wait()

        columns = pl.ds(pl.multiple_of(spot * D, D), D)
        if part == 0:
            go(wide.at[slot], one.at[rows, columns])
        elif part == 1:
            go(split.at[slot], two.at[:, spot % 2, spot // 2, :, rows])
        else:

            @pl.when(spot < 3)
            def _():
                go(wide.at[slot], qkv.at[rows, columns])

            @pl.when(spot == 3)
            def _():
                go(wide.at[slot], proj.at[rows, :])

    for i in range(min(SLOTS, len(tasks))):
        load(i).start()
    for i in range(len(tasks)):
        part = tasks[i][0]
        slot = i % SLOTS
        load(i).wait()
        if i >= SLOTS:
            store(i - SLOTS, False)
        high = PIECE[2]
        core = core_of(i)
        for outer in range(PIECE[0]):
            for inner in range(PIECE[1]):
                piece = raw[slot, outer, inner].astype(f32)
                if part == 0:
                    y, z = at[1] ^ hop_of(outer, core), at[2] ^ hop_of(inner, core)
                    start = pl.multiple_of((y // 2 * 4 + z) * high, high)
                    column = pl.multiple_of(y % 2 * HID, HID)
                    wide[slot, pl.ds(start, high), pl.ds(column, HID)] = piece
                elif part == 1:
                    x, z = at[0] ^ hop_of(outer, core), at[2] ^ hop_of(inner, core)
                    split[slot, x, pl.ds(pl.multiple_of(z * high, high), high)] = piece
                else:
                    y, x = at[1] ^ hop_of(outer, core), at[0] ^ hop_of(inner, core)
                    start = pl.multiple_of((x * 2 + y % 2) * COLS + y // 2 * high, high)
                    tall[pl.ds(start, high)] = piece
        if part == 2:
            wide[slot] = jnp.transpose(tall[...])
        store(i, True)
        if i + SLOTS < len(tasks):
            load(i + SLOTS).start()
    for i in range(max(0, len(tasks) - SLOTS), len(tasks)):
        store(i, False)


def place_pieces(info, pieces, old):
    tasks, arrays = [], []
    for part, mine, other, hop in pieces:
        for swapped, array in ((False, mine), (True, other)):
            place = [i for i, held in enumerate(arrays) if held is array]
            if not place:
                place = [len(arrays)]
                arrays.append(array)
            tasks.append((part, place[0], hop, swapped))
    sds = jax.ShapeDtypeStruct
    shapes = [
        sds((D, FF), f32),
        sds((4, 2, 2, HID // 2, D), f32),
        sds((D, 3 * D), f32),
        sds((D, D), f32),
    ]
    anywhere = pl.BlockSpec(memory_space=pl.ANY)
    n_old = len(old)

    def body(*refs):
        place_kernel(tasks, len(arrays), n_old, *refs)

    return pl.pallas_call(
        body,
        grid_spec=pltpu.PrefetchScalarGridSpec(
            num_scalar_prefetch=1,
            grid=(1,),
            in_specs=[anywhere] * (len(arrays) + n_old),
            out_specs=[anywhere] * 4,
            scratch_shapes=[
                pltpu.VMEM((SLOTS,) + PIECE, bf16),
                pltpu.VMEM((SLOTS, HID, D), f32),
                pltpu.VMEM((SLOTS, 4, HID // 2, HID), f32),
                pltpu.VMEM((D, HID), f32),
                pltpu.SemaphoreType.DMA((SLOTS,)),
                pltpu.SemaphoreType.DMA((SLOTS,)),
            ],
        ),
        out_shape=shapes,
        input_output_aliases={1 + len(arrays) + i: i for i in range(n_old)},
        compiler_params=pltpu.CompilerParams(vmem_limit_bytes=PLACE_LIMIT),
        cost_estimate=pl.CostEstimate(
            flops=0, bytes_accessed=1800000 * len(tasks), transcendentals=0
        ),
    )(info, *arrays, *old)


def vector_kernel(info, gathered, *refs):
    outs, flat = refs[:9], refs[9]
    for outer in range(2):
        for inner in range(4):
            y = info[AT_Y] ^ hop_of(outer, info[CORE])
            x = info[AT_X] ^ hop_of(inner, info[CORE])
            flat[x * 2 + y % 2] = gathered[outer, inner].astype(f32)
    shared = jnp.sum(flat[...], axis=0)
    for i in range(5):
        outs[i][:HID] = shared[2 * i]
        outs[i][HID:] = shared[2 * i + 1]
    for j in range(TP):
        outs[5][j * HID : (j + 1) * HID] = flat[j, 10]
    total = jnp.zeros((VEC_ROWS, D), f32)
    source = lax.broadcasted_iota(jnp.int32, (PAIR, D), 0)
    target = lax.broadcasted_iota(jnp.int32, (PAIR, D), 1)
    for j in range(TP):
        moves = (source + j * COLS == target) & (source < COLS)
        total += dot(flat[j, :, :PAIR].astype(bf16), moves.astype(bf16), ((1,), (0,)))
    for i in range(3):
        outs[6 + i][...] = total[11 + i]


def place_vectors(info, gathered):
    block = (2, 4, VEC_ROWS, HID)
    last = gathered.shape[2] // VEC_ROWS - 1
    return launch(
        vector_kernel,
        (1,),
        info,
        [(gathered, pl.BlockSpec(block, lambda i, _: (0, 0, last, 0)))],
        [made((D,), f32)] * 5 + [made((FF,), f32)] + [made((D,), f32)] * 3,
        [pltpu.VMEM((TP, VEC_ROWS, HID), f32)],
        10**7,
        10**6,
    )


def per_device(
    layer_input,
    out_grad,
    lengths,
    keep,
    ln1_gain,
    ln1_bias,
    w_qkv,
    b_query,
    b_value,
    w_proj,
    b_proj,
    ln2_gain,
    ln2_bias,
    w_fc1,
    b_fc1,
    w_fc2,
    b_fc2,
):
    _, tokens, width = layer_input.shape
    row = tokens * TP
    group = lax.axis_index(BLK)
    places = [
        group,
        lax.axis_index("c"),
        lax.axis_index("x"),
        lax.axis_index(("yh", "yl")),
        lax.axis_index("z"),
        lax.axis_index("yl"),
        first_head(group),
        group % 2 * (HEAD_DIM // 2),
    ]
    info = jnp.concatenate(
        [jnp.cumsum(lengths[0]), keep[0, 0], keep[1, 0], jnp.stack(places).astype(jnp.int32)]
    )
    axis_x, axis_y, axis_z = ("c", "x"), ("yh", "c", "yl"), ("z", "c")

    x_all = spread(layer_input[0], BLK, TP)
    grad_z_all = spread(out_grad[0], BLK, TP)
    x_all = x_all.reshape(row, width)
    attended, h_all, xhat_all = attend(
        info, x_all, ln1_gain, ln1_bias, w_qkv, b_query, b_value, tokens
    )
    by_yl = exchange(attended, ("x", "yl"), None)
    output, grad_mid, outgoing, sums_two = mlp(
        info,
        attended,
        layer_input[0],
        out_grad[0],
        w_proj,
        b_proj,
        ln2_gain,
        ln2_bias,
        w_fc1,
        b_fc1,
        w_fc2,
        b_fc2,
    )
    by_yl, outgoing, grad_z_all = lax.optimization_barrier((by_yl, outgoing, grad_z_all))
    incoming = lax.all_to_all(outgoing, BLK, 0, 0)
    attended_all = jnp.stack([attended, by_yl])[None]
    beside = exchange(attended_all, axis_x, (1, 3))
    pair = pair_forward(info, h_all, w_qkv, b_query, b_value)
    beside, pair = lax.optimization_barrier((beside, tuple(pair)))
    attended_all = jnp.concatenate([attended_all, beside])
    attended_far = exchange(attended_all, axis_x, (3, 1))
    grad_qkv, back_out, sums_one = pair_back(info, incoming, *pair, h_all, xhat_all)
    mine, other = hidden_grads(
        info,
        attended_all,
        attended_far,
        x_all,
        grad_z_all.reshape(row, width),
        incoming,
        w_proj,
        b_proj,
        ln2_gain,
        ln2_bias,
        w_fc1,
        b_fc1,
        w_fc2,
        grad_qkv,
        sums_one,
        sums_two,
    )
    back_in = lax.all_to_all(back_out, BLK, 0, 0)
    mine, other, back_in = lax.optimization_barrier((mine, other, back_in))

    half = (mine.astype(f32) + swap_core(other).astype(f32)).astype(bf16)
    pieces = lax.all_to_all(half, ("yh", "z"), 0, 0)
    x_grad = input_grad(info, back_in, w_qkv, layer_input[0], grad_mid, ln1_gain)
    pieces, x_grad = lax.optimization_barrier((pieces, x_grad))
    piece = jnp.sum(pieces.astype(f32), axis=0).astype(bf16)
    high = HID // TP
    one_two, part_b = together([piece[: 2 * high], piece[2 * high :]], [axis_z, axis_x])
    along_y = jnp.concatenate([one_two[:, :high], part_b], axis=1)
    fence = lax.optimization_barrier
    along_y, part_two = along_y[None], one_two[None, :, high:]
    got_y, got_x = fence((exchange(along_y, axis_y, (1, 3)), exchange(part_two, axis_x, (1, 3))))
    along_y, part_two = jnp.concatenate([along_y, got_y]), jnp.concatenate([part_two, got_x])
    vectors = tuple(place_vectors(info, along_y))
    along_y = along_y[:, :, : 2 * high]
    got_y, got_x, vectors = fence(
        (exchange(along_y, axis_y, (3, 1)), exchange(part_two, axis_x, (3, 1)), vectors)
    )
    along_y, part_two = jnp.concatenate([along_y, got_y]), jnp.concatenate([part_two, got_x])
    parts = (along_y[:, :, :high], part_two, along_y[:, :, high:])
    axes = (axis_x, axis_y, axis_z)

    def place(stage, old):
        return place_pieces(
            info, [(i, p, q, hop) for held, swapped, hop in stage for i, (p, q) in enumerate(zip(held, swapped))], old
        )

    def hop(pieces, by_core):
        return [exchange(p, axis, by_core) for p, axis in zip(pieces, axes)]

    def swapped(pieces):
        return [swap_core(p) for p in pieces]

    beside = [swap_core(jnp.stack(parts))] * 3
    near, far = hop(parts, (1, 3)), hop(parts, (3, 1))
    outs = tuple(place([(parts, beside, 0)], ()))
    near, far[0], far[1], outs = fence((near, far[0], far[1], outs))
    last, near_beside = hop(near, (3, 1)), swapped(near)
    outs = tuple(place([(near, near_beside, 1)], outs))
    far, outs = fence((far, outs))
    far_beside = swapped(far)
    last, far_beside, outs = fence((last, far_beside, outs))
    last_beside = swapped(last)
    outs = tuple(place([(far, far_beside, 2)], outs))
    last_beside, outs = fence((last_beside, outs))
    outs = place([(last, last_beside, 3)], outs)
    grad_w_fc1, grad_w_fc2, grad_w_qkv, grad_w_proj = outs

    ln1g, ln1b, ln2g, ln2b, b_two_grad, b_one_grad, bq_grad, bv_grad, b_proj_grad = vectors
    return (
        output[None],
        x_grad[None],
        ln1g,
        ln1b,
        grad_w_qkv,
        bq_grad,
        bv_grad,
        grad_w_proj,
        b_proj_grad,
        ln2g,
        ln2b,
        grad_w_fc1,
        b_one_grad,
        grad_w_fc2.reshape(FF, D),
        b_two_grad,
    )


def solution(mesh):
    fine = Mesh(mesh.devices.reshape(2, 4, 2, 4, 2), ("yh", "z", "c", "x", "yl"))
    dp = ("yh", "z", "c")
    tokens = P(dp, BLK, None)
    placed = (tokens, tokens, P(dp, None), P(None, dp, None)) + (P(),) * 13
    return jax.shard_map(
        per_device,
        mesh=fine,
        in_specs=placed,
        out_specs=(tokens, tokens) + (P(),) * 13,
        check_vma=False,
    )
```
